128 devices in a mesh: dp: 8 (over y, core), tile: 16 (over z, x).
Axes of the slice: x: 4, y: 4, z: 4, core: 2. Of those that a mesh axis runs over, the one named last changes fastest.
Arguments:
- gate_pre: bfloat16 [3072, 14336], P('dp', 'tile'), may hold values from -6 to 6
- up_pre: bfloat16 [3072, 14336], P('dp', 'tile'), may hold values from -6 to 6
- grad_hidden: bfloat16 [3072, 14336], P('dp', 'tile'), may hold values from -6 to 6
- doc_tokens: int32 [32], replicated, may hold values from 1 to 381, as said below
- doc_shard: int32 [32], replicated, may hold values from 0 to 7, as said below
Outputs:
- act_factor: float32 [14336, 8, 1792], P('tile', 'dp')
- grad_factor: float32 [14336, 8, 1792], P('tile', 'dp')
The draws below stay inside these ranges and needn't reach their ends.
Inputs may be any that keep to these rules, and one draw needn't show every extreme that they name: `doc_tokens`: each data shard holds exactly 4 documents whose tokens together fill its first slots; the documents of one shard total at most 384 tokens, exactly 384 on one shard, and all documents together hold 2048 tokens. One document holds exactly 381 tokens. `doc_shard`: each data shard index appears exactly 4 times.
All inputs are finite; a program needn't handle non-finite values.
Results may differ from the reference program's by a relative error of at most 0.0039.
Values may be sent and summed in bfloat16 or wider, within the bound.
A program may use at most 128 MiB of HBM per device.

```python
import jax
import jax.numpy as jnp

FF = 14336
TOK_DEV = 256
DOCS_SHARD = 4
CAP = 384
SLOTS = 3072
TOKENS = 2048
N_DP = 8
N_TILE = 16


def document_plan(key):
    key_heavy, key_extra, key_cuts, key_order = jax.random.split(key, 4)
    owners = jnp.arange(N_DP, dtype=jnp.int32)
    heaviest = jax.random.randint(key_heavy, (), 0, N_DP)
    extra_total = TOK_DEV * N_DP // 2 - TOK_DEV
    chosen = jax.random.permutation(key_extra, (N_DP - 1) * TOK_DEV)[:extra_total]
    others = chosen // TOK_DEV
    targets = others + (others >= heaviest).astype(jnp.int32)
    extras = jnp.sum((targets[:, None] == owners[None, :]).astype(jnp.int32), axis=0)
    shard_loads = jnp.where(owners == heaviest, CAP, TOK_DEV // 2 + extras)
    cut_points = jax.random.randint(key_cuts, (N_DP, DOCS_SHARD - 1), 0, (shard_loads - DOCS_SHARD + 1)[:, None])
    cut_points = jnp.where((owners == heaviest)[:, None], 0, cut_points)
    cut_points = jnp.sort(cut_points, axis=1)
    edges = jnp.concatenate([jnp.zeros((N_DP, 1), jnp.int32), cut_points, (shard_loads - DOCS_SHARD)[:, None]], axis=1)
    lengths = (edges[:, 1:] - edges[:, :-1] + 1).reshape(-1)
    holders = jnp.repeat(owners, DOCS_SHARD)
    order = jax.random.permutation(key_order, N_DP * DOCS_SHARD)
    doc_tokens = jnp.zeros((N_DP * DOCS_SHARD,), jnp.int32).at[order].set(lengths)
    doc_shard = jnp.zeros((N_DP * DOCS_SHARD,), jnp.int32).at[order].set(holders)
    return (doc_tokens, doc_shard)


def draw_doc_tokens(key, part):
    return document_plan(key)[0]


def draw_doc_shard(key, part):
    return document_plan(key)[1]


def block_scale(rng, shape, cuts, smallest, high):
    def one(position, shards_of):
        heights = jax.random.uniform(jax.random.fold_in(jax.random.fold_in(rng, 6), position), (shards_of,), jnp.float32, smallest / len(cuts), high / len(cuts))
        return jnp.repeat(jnp.exp(heights), shape[position] // shards_of).reshape((-1,) + (1,) * (len(shape) - position - 1))

    factor_of = one(*cuts[0])
    for cut in cuts[1:]:
        factor_of = factor_of * one(*cut)
    return factor_of


def bell_draw(key, dims, spread, bound, pieces=(), kind=jnp.bfloat16):
    result = jax.random.normal(key, dims, jnp.float32) * spread
    if len(pieces) > 0:
        result = block_scale(key, dims, pieces, -0.22, 0.18) * result
    return jnp.clip(result, min=-bound, max=bound).astype(kind)


def setup_inputs(seed: int = 0) -> dict:
    seeds = jax.random.split(jax.random.key(seed), 6)
    gate_pre = bell_draw(seeds[0], (SLOTS, FF), 1.0, 6.0, ((0, 8), (1, 16)))
    up_pre = bell_draw(seeds[1], (SLOTS, FF), 1.0, 6.0, ((0, 8), (1, 16)))
    grad_hidden = bell_draw(seeds[2], (SLOTS, FF), 1.0, 6.0, ((0, 8), (1, 16)))
    doc_tokens = draw_doc_tokens(jax.random.fold_in(seeds[5], 71), 0)
    doc_shard = draw_doc_shard(jax.random.fold_in(seeds[5], 71), 0)
    return dict(gate_pre=gate_pre, up_pre=up_pre, grad_hidden=grad_hidden, doc_tokens=doc_tokens, doc_shard=doc_shard)


def loads_of(doc_tokens, doc_shard):
    owners = jnp.arange(N_DP, dtype=jnp.int32)
    return jnp.sum(jnp.where(doc_shard[None, :] == owners[:, None], doc_tokens[None, :], 0), axis=1)


def arrange(square):
    group = FF // (N_TILE * N_DP)
    return square.reshape(FF, N_TILE, N_DP, group).transpose(0, 2, 1, 3).reshape(FF, N_DP, FF // N_DP)


def reference(gate_pre, up_pre, grad_hidden, doc_tokens, doc_shard):
    owners = jnp.arange(N_DP, dtype=jnp.int32)
    shard_loads = loads_of(doc_tokens, doc_shard)
    slot_index = jnp.arange(N_DP * CAP, dtype=jnp.int32)
    owner_rows = slot_index // CAP
    within = slot_index % CAP
    limits = jnp.sum(jnp.where(owner_rows[:, None] == owners[None, :], shard_loads[None, :], 0), axis=1)
    live_rows = (within < limits)[:, None]
    gate_float = gate_pre.astype(jnp.float32)
    up_float = up_pre.astype(jnp.float32)
    grad_float = grad_hidden.astype(jnp.float32)
    sigmoid_gate = jax.nn.sigmoid(gate_float)
    hidden = jnp.where(live_rows, gate_float * sigmoid_gate * up_float, 0.0).astype(jnp.bfloat16)
    dgate = jnp.where(live_rows, grad_float * up_float * sigmoid_gate * (1.0 + gate_float * (1.0 - sigmoid_gate)), 0.0).astype(jnp.bfloat16)
    scale_factor = 1.0 / TOKENS
    act_factor = arrange(jnp.dot(hidden.T, hidden, preferred_element_type=jnp.float32) * scale_factor)
    grad_factor = arrange(jnp.dot(dgate.T, dgate, preferred_element_type=jnp.float32) * scale_factor)
    return act_factor, grad_factor
```

```python
import jax
import jax.numpy as jnp
from jax import lax
from jax.experimental import pallas as pl
from jax.experimental.pallas import tpu as pltpu
from jax.sharding import PartitionSpec as P

MESH = pl.DeviceIdType.MESH
TOK_DEV = 256
DOCS_SHARD = 4
WIDE = 256
SIDE = 4


def packing_blocks(shards, capacity, tokens):
    blocks = [[] for _ in range(tokens // WIDE)]
    for shard in range(shards):
        after = shards - shard
        first = max(DOCS_SHARD * shard, tokens - capacity * after)
        last = min(capacity * shard, tokens - DOCS_SHARD * after) + capacity
        for block in range(first // WIDE, -(-min(last, tokens) // WIDE)):
            blocks[block].append(shard)
    return blocks


def make_kernel(capacity, units, group, shards, tiles):
    tokens = TOK_DEV * shards
    blocks = packing_blocks(shards, capacity, tokens)
    slots = {}
    for n, members in enumerate(blocks):
        for shard in members:
            slots[n, shard] = len(slots)
    pieces = 4
    width = tokens // pieces
    columns = tiles * group

    def kernel(tok_ref, own_ref, gate_ref, up_ref, down_ref, act_ref, grad_ref, xt, rv, perm, rp, cp,
               swap_s, swap_r, local_s, row_s, row_r, col_s, col_r):
        outs = (act_ref, grad_ref)
        dp, tile = lax.axis_index("dp"), lax.axis_index("tile")
        y, core = dp // 2, lax.rem(dp, 2)
        z, x = tile // SIDE, lax.rem(tile, SIDE)

        def plus(a, d):
            return lax.rem(a + d + SIDE, SIDE)

        def over_dp(offset):
            return lax.rem(dp + offset + shards, shards)

        def y_peer(d):
            return (plus(y, d) * 2 + core, tile)

        sibling = (y * 2 + 1 - core, tile)

        def plane(first_is_x, d1, d2):
            dx, dz = (d1, d2) if first_is_x else (d2, d1)
            return plus(z, dz) * SIDE + plus(x, dx)

        barrier = pltpu.get_barrier_semaphore()
        peers = [(over_dp(o), tile) for o in range(1, shards)]
        peers += [(dp, plane(True, d, 0)) for d in (1, 2, 3)] + [(dp, plane(True, 0, d)) for d in (1, 2, 3)]
        for peer in peers:
            pl.semaphore_signal(barrier, inc=1, device_id=peer, device_id_type=MESH)

        def count(i, loads):
            return tuple(v + jnp.where(own_ref[i] == j, tok_ref[i], 0) for j, v in enumerate(loads))

        loads = lax.fori_loop(0, shards * DOCS_SHARD, count, (jnp.int32(0),) * shards)
        own_load, offsets, total = jnp.int32(0), [], jnp.int32(0)
        for j in range(shards):
            own_load = own_load + jnp.where(dp == j, loads[j], 0)
            offsets.append(total)
            total = total + loads[j]

        live = lax.broadcasted_iota(jnp.int32, (capacity, 128), 0) < own_load

        def make_hidden(b, _):
            cols = pl.ds(pl.multiple_of(b * 128, 128), 128)
            g = gate_ref[:, cols].astype(jnp.float32)
            u = up_ref[:, cols].astype(jnp.float32)
            h = jnp.where(live, g * jax.nn.sigmoid(g) * u, 0.0)
            xt[0, cols, :] = h.T.astype(jnp.bfloat16)
            return 0

        def make_dgate(b, _):
            cols = pl.ds(pl.multiple_of(b * 128, 128), 128)
            g = gate_ref[:, cols].astype(jnp.float32)
            u = up_ref[:, cols].astype(jnp.float32)
            d = down_ref[:, cols].astype(jnp.float32)
            s = jax.nn.sigmoid(g)
            h = jnp.where(live, d * u * s * (1.0 + g * (1.0 - s)), 0.0)
            xt[1, cols, :] = h.T.astype(jnp.bfloat16)
            return 0

        def at_group(index):
            return pl.ds(pl.multiple_of(index * group, 16), group)

        def swap(f, o):
            return pltpu.make_async_remote_copy(
                src_ref=xt.at[f, at_group(over_dp(o))], dst_ref=rv.at[f, dp],
                send_sem=swap_s.at[f, o], recv_sem=swap_r.at[f, o],
                device_id=(over_dp(o), tile), device_id_type=MESH)

        def swap_in(f, o):
            return pltpu.make_async_remote_copy(
                src_ref=xt.at[f, at_group(dp)], dst_ref=rv.at[f, over_dp(-o)],
                send_sem=swap_s.at[f, o], recv_sem=swap_r.at[f, o],
                device_id=(over_dp(o), tile), device_id_type=MESH)

        def swap_own(f):
            return pltpu.make_async_copy(xt.at[f, at_group(dp)], rv.at[f, dp], local_s.at[f])

        def start_swap(f):
            for o in (3, 4, 5, 2, 6, 7, 1):
                swap(f, o).start()
            swap_own(f).start()

        def end_swap(f):
            swap_own(f).wait()
            for o in range(1, shards):
                swap_in(f, o).wait_recv()

        def build_perm():
            diff = (lax.broadcasted_iota(jnp.int32, (capacity, WIDE), 1)
                    - lax.broadcasted_iota(jnp.int32, (capacity, WIDE), 0))
            for (n, shard), slot in slots.items():
                hit = diff == offsets[shard] - n * WIDE
                perm[slot] = jnp.where(hit, 1.0, 0.0).astype(jnp.bfloat16)

        def pack(f, q):
            for n in range(q * width // WIDE, (q + 1) * width // WIDE):
                acc = None
                for shard in blocks[n]:
                    term = jnp.dot(rv[f, shard], perm[slots[n, shard]], preferred_element_type=jnp.float32)
                    acc = term if acc is None else acc + term
                packed = acc.astype(jnp.bfloat16)
                cp[f, at_group(tile), n * WIDE:(n + 1) * WIDE] = packed
                rp[f, at_group(dp), n * WIDE:(n + 1) * WIDE] = packed

        def row(f, index, origin, peer):
            part = rp.at[f, at_group(origin)]
            return pltpu.make_async_remote_copy(
                src_ref=part, dst_ref=part, send_sem=row_s.at[f, index], recv_sem=row_r.at[f, index],
                device_id=peer, device_id_type=MESH)

        def row_out(f):
            for d in (1, 2, 3):
                row(f, d, dp, y_peer(d)).start()
            row(f, 0, dp, sibling).start()

        def row_pass(f):
            for d in (1, 3, 2):
                origin = plus(y, -d) * 2 + core
                row(f, d, origin, y_peer(d)).wait_recv()
                row(f, SIDE + d, origin, sibling).start()

        def row_end(f):
            for d in range(SIDE):
                index = 0 if d == 0 else SIDE + d
                row(f, index, plus(y, -d) * 2 + 1 - core, sibling).wait_recv()

        def column(f, q, index, origin, peer):
            part = cp.at[f, at_group(origin), pl.ds(q * width, width)]
            return pltpu.make_async_remote_copy(
                src_ref=part, dst_ref=part, send_sem=col_s.at[f, q, index], recv_sem=col_r.at[f, q, index],
                device_id=(dp, peer), device_id_type=MESH)

        def col_out(f, q):
            first = q % 2 == 0
            for d in (1, 3, 2):
                column(f, q, d - 1, tile, plane(first, d, 0)).start()
            for d in (1, 3, 2):
                column(f, q, 2 + d, tile, plane(first, 0, d)).start()

        def col_pass(f, q):
            first = q % 2 == 0
            for b in (1, 3, 2):
                origin = plane(first, -b, 0)
                column(f, q, b - 1, origin, plane(first, b, 0)).wait_recv()
                for d in (1, 3, 2):
                    column(f, q, 2 + b * 3 + d, origin, plane(first, 0, d)).start()

        def col_end(f, q):
            first = q % 2 == 0
            for b in range(SIDE):
                for d in (1, 2, 3):
                    column(f, q, 2 + b * 3 + d, plane(first, -b, -d), plane(first, 0, d)).wait_recv()

        def multiply(f, pair):
            ks = pl.ds(pair * 2 * width, 2 * width)

            def step(n, _):
                cols = pl.ds(pl.multiple_of(n * WIDE, WIDE), WIDE)
                gram = lax.dot_general(rp[f, :, ks], cp[f, cols, ks], (((1,), (1,)), ((), ())),
                                       preferred_element_type=jnp.float32)
                if pair == 0:
                    outs[f][:, cols] = gram
                else:
                    outs[f][:, cols] = (outs[f][:, cols] + gram) * (1.0 / tokens)
                return 0

            lax.fori_loop(0, columns // WIDE, step, 0)

        lax.fori_loop(0, units // 128, make_hidden, 0)
        pl.semaphore_wait(barrier, len(peers))
        start_swap(0)
        lax.fori_loop(0, units // 128, make_dgate, 0)
        build_perm()
        end_swap(0)
        start_swap(1)
        pack(0, 0)
        col_out(0, 0)
        pack(0, 1)
        col_out(0, 1)
        pack(0, 2)
        pack(0, 3)
        col_pass(0, 0)
        col_pass(0, 1)
        col_out(0, 2)
        col_out(0, 3)
        end_swap(1)
        row_out(0)
        for q in range(pieces):
            pack(1, q)
        col_pass(0, 2)
        col_pass(0, 3)
        col_out(1, 0)
        col_out(1, 1)
        row_pass(0)
        row_out(1)
        row_end(0)
        col_end(0, 0)
        col_end(0, 1)
        multiply(0, 0)
        col_pass(1, 0)
        col_pass(1, 1)
        col_out(1, 2)
        col_out(1, 3)
        col_end(0, 2)
        col_end(0, 3)
        multiply(0, 1)
        col_pass(1, 2)
        col_pass(1, 3)
        row_pass(1)
        row_end(1)
        col_end(1, 0)
        col_end(1, 1)
        multiply(1, 0)
        col_end(1, 2)
        col_end(1, 3)
        multiply(1, 1)

        for f in range(2):
            for o in range(1, shards):
                swap(f, o).wait_send()
            for d in range(2 * SIDE):
                if d != SIDE:
                    row(f, d, dp, sibling).wait_send()
            for q in range(pieces):
                for i in range(15):
                    column(f, q, i, tile, plane(True, 1, 0)).wait_send()

    scratch = [
        pltpu.VMEM((2, units, capacity), jnp.bfloat16),
        pltpu.VMEM((2, shards, group, capacity), jnp.bfloat16),
        pltpu.VMEM((len(slots), capacity, WIDE), jnp.bfloat16),
        pltpu.VMEM((2, units, tokens), jnp.bfloat16),
        pltpu.VMEM((2, columns, tokens), jnp.bfloat16),
        pltpu.SemaphoreType.DMA((2, shards)),
        pltpu.SemaphoreType.DMA((2, shards)),
        pltpu.SemaphoreType.DMA((2,)),
        pltpu.SemaphoreType.DMA((2, 2 * SIDE)),
        pltpu.SemaphoreType.DMA((2, 2 * SIDE)),
        pltpu.SemaphoreType.DMA((2, pieces, 15)),
        pltpu.SemaphoreType.DMA((2, pieces, 15)),
    ]
    return kernel, scratch


def solution(mesh):
    shards, tiles = mesh.shape["dp"], mesh.shape["tile"]

    def on_device(gate_pre, up_pre, grad_hidden, doc_tokens, doc_shard):
        capacity, units = gate_pre.shape
        group = units // shards
        kernel, scratch = make_kernel(capacity, units, group, shards, tiles)
        columns = tiles * group
        smem, vmem = pl.BlockSpec(memory_space=pltpu.SMEM), pl.BlockSpec(memory_space=pltpu.VMEM)
        act, grad = pl.pallas_call(
            kernel,
            out_shape=[jax.ShapeDtypeStruct((units, columns), jnp.float32)] * 2,
            in_specs=[smem, smem, vmem, vmem, vmem],
            out_specs=[vmem, vmem],
            scratch_shapes=scratch,
            compiler_params=pltpu.CompilerParams(
                collective_id=0, has_side_effects=True, vmem_limit_bytes=58 << 20),
            name="gram_exchange",
        )(doc_tokens, doc_shard, gate_pre, up_pre, grad_hidden)
        return act.reshape(units, 1, columns), grad.reshape(units, 1, columns)

    return jax.shard_map(
        on_device,
        mesh=mesh,
        in_specs=(P("dp", "tile"), P("dp", "tile"), P("dp", "tile"), P(), P()),
        out_specs=(P("tile", "dp", None), P("tile", "dp", None)),
        check_vma=False,
    )
```

```python
import jax
import jax.numpy as jnp
from jax import lax
from jax.experimental import pallas as pl
from jax.experimental.pallas import tpu as pltpu
from jax.sharding import PartitionSpec as P

MESH = pl.DeviceIdType.MESH
TOK_DEV = 256
DOCS_SHARD = 4
F1_WIDTHS = (512, 256, 256)
WIDE = 256
SIDE = 4


def packing_blocks(shards, capacity, tokens):
    blocks = [[] for _ in range(tokens // WIDE)]
    for shard in range(shards):
        after = shards - shard
        first = max(DOCS_SHARD * shard, tokens - capacity * after)
        last = min(capacity * shard, tokens - DOCS_SHARD * after) + capacity
        for block in range(first // WIDE, -(-min(last, tokens) // WIDE)):
            blocks[block].append(shard)
    return blocks


def make_kernel(capacity, units, group, shards, tiles):
    tokens = TOK_DEV * shards
    blocks = packing_blocks(shards, capacity, tokens)
    slots = {}
    for n, members in enumerate(blocks):
        for shard in members:
            slots[n, shard] = len(slots)
    half = tokens // 2
    cut = group * 3 // 7
    parts = [(0, 0, cut), (0, cut, group - cut), (1, 0, group)]
    pieces = []
    for f, top, rows in parts[:2]:
        pieces += [(f, top, rows, 0, half), (f, top, rows, half, half)]
    start = 0
    for wide in F1_WIDTHS:
        pieces += [(1, 0, group, start, wide), (1, 0, group, start + wide, wide)]
        start += 2 * wide
    pairs = [(i, i + 1) for i in range(0, len(pieces), 2)]
    columns = tiles * group

    def kernel(tok_ref, own_ref, gate_ref, up_ref, down_ref, act_ref, grad_ref, rp1, cp1, xt, rv, perm, rp0, cp0,
               swap_s, swap_r, local_s, row_s, row_r, col_s, col_r):
        outs, rp, cp = (act_ref, grad_ref), (rp0, rp1), (cp0, cp1)
        sent = []

        def send(copy):
            copy.start()
            sent.append(copy)

        dp, tile = lax.axis_index("dp"), lax.axis_index("tile")
        y, core = dp // 2, lax.rem(dp, 2)
        z, x = tile // SIDE, lax.rem(tile, SIDE)

        def plus(a, d):
            return lax.rem(a + d + SIDE, SIDE)

        def over_dp(offset):
            return lax.rem(dp + offset + shards, shards)

        def y_peer(d):
            return (plus(y, d) * 2 + core, tile)

        sibling = (y * 2 + 1 - core, tile)

        def plane(first_is_x, d1, d2):
            dx, dz = (d1, d2) if first_is_x else (d2, d1)
            return plus(z, dz) * SIDE + plus(x, dx)

        barrier = pltpu.get_barrier_semaphore()
        peers = [(over_dp(o), tile) for o in range(1, shards)]
        peers += [(dp, plane(True, d, 0)) for d in (1, 2, 3)] + [(dp, plane(True, 0, d)) for d in (1, 2, 3)]
        for peer in peers:
            pl.semaphore_signal(barrier, inc=1, device_id=peer, device_id_type=MESH)

        def count(i, loads):
            return tuple(v + jnp.where(own_ref[i] == j, tok_ref[i], 0) for j, v in enumerate(loads))

        loads = lax.fori_loop(0, shards * DOCS_SHARD, count, (jnp.int32(0),) * shards)
        own_load, offsets, total = jnp.int32(0), [], jnp.int32(0)
        for j in range(shards):
            own_load = own_load + jnp.where(dp == j, loads[j], 0)
            offsets.append(total)
            total = total + loads[j]

        live = lax.broadcasted_iota(jnp.int32, (capacity, 128), 0) < own_load

        def make_hidden(b, _):
            cols = pl.ds(pl.multiple_of(b * 128, 128), 128)
            g = gate_ref[:, cols].astype(jnp.float32)
            u = up_ref[:, cols].astype(jnp.float32)
            h = jnp.where(live, g * jax.nn.sigmoid(g) * u, 0.0)
            xt[0, cols, :] = h.T.astype(jnp.bfloat16)
            return 0

        def make_dgate(b, _):
            cols = pl.ds(pl.multiple_of(b * 128, 128), 128)
            g = gate_ref[:, cols].astype(jnp.float32)
            u = up_ref[:, cols].astype(jnp.float32)
            d = down_ref[:, cols].astype(jnp.float32)
            s = jax.nn.sigmoid(g)
            h = jnp.where(live, d * u * s * (1.0 + g * (1.0 - s)), 0.0)
            xt[1, cols, :] = h.T.astype(jnp.bfloat16)
            return 0

        def at_group(index):
            return pl.ds(pl.multiple_of(index * group, 16), group)

        def rows_of(index, top, rows):
            return pl.ds(pl.multiple_of(index * group + top, 16), rows)

        def swap(part, o, source, home):
            f, top, rows = parts[part]
            return pltpu.make_async_remote_copy(
                src_ref=xt.at[f, rows_of(home, top, rows)], dst_ref=rv.at[f, source, pl.ds(top, rows)],
                send_sem=swap_s.at[part, o], recv_sem=swap_r.at[part, o],
                device_id=(over_dp(o), tile), device_id_type=MESH)

        def swap_own(part):
            f, top, rows = parts[part]
            return pltpu.make_async_copy(
                xt.at[f, rows_of(dp, top, rows)], rv.at[f, dp, pl.ds(top, rows)], local_s.at[part])

        def start_swap(part):
            for o in (3, 4, 5, 2, 6, 7, 1):
                send(swap(part, o, dp, over_dp(o)))
            swap_own(part).start()

        def end_swap(part):
            swap_own(part).wait()
            for o in range(1, shards):
                swap(part, o, over_dp(-o), dp).wait_recv()

        def build_perm():
            diff = (lax.broadcasted_iota(jnp.int32, (capacity, WIDE), 1)
                    - lax.broadcasted_iota(jnp.int32, (capacity, WIDE), 0))
            for (n, shard), slot in slots.items():
                hit = diff == offsets[shard] - n * WIDE
                perm[slot] = jnp.where(hit, 1.0, 0.0).astype(jnp.bfloat16)

        def pack(piece):
            f, top, rows, start, wide = pieces[piece]
            for n in range(start // WIDE, (start + wide) // WIDE):
                acc = None
                for shard in blocks[n]:
                    term = jnp.dot(rv[f, shard, top:top + rows], perm[slots[n, shard]],
                                   preferred_element_type=jnp.float32)
                    acc = term if acc is None else acc + term
                packed = acc.astype(jnp.bfloat16)
                cp[f][rows_of(tile, top, rows), n * WIDE:(n + 1) * WIDE] = packed
                rp[f][rows_of(dp, top, rows), n * WIDE:(n + 1) * WIDE] = packed

        def row(f, index, origin, peer):
            lanes = pl.ds((index - 2) * half, half) if index in (2, 3) else slice(None)
            part = rp[f].at[at_group(origin), lanes]
            return pltpu.make_async_remote_copy(
                src_ref=part, dst_ref=part, send_sem=row_s.at[f, index], recv_sem=row_r.at[f, index],
                device_id=peer, device_id_type=MESH)

        def same_core(d):
            return plus(y, d) * 2 + core

        def row_out(f):
            send(row(f, 0, dp, y_peer(1)))
            send(row(f, 1, dp, y_peer(-1)))
            send(row(f, 4, dp, sibling))

        def row_pass(f):
            for index, d in ((0, 1), (1, -1)):
                row(f, index, same_core(-d), sibling).wait_recv()
                send(row(f, 2 + index, same_core(-d), y_peer(d)))
                send(row(f, 5 + index, same_core(-d), sibling))

        def row_far(f):
            for index in (2, 3):
                row(f, index, same_core(2), sibling).wait_recv()
            send(row(f, 7, same_core(2), sibling))

        def row_end(f):
            for index, d in ((4, 0), (5, -1), (6, 1), (7, 2)):
                row(f, index, plus(y, d) * 2 + 1 - core, sibling).wait_recv()

        def column(piece, index, origin, peer):
            f, top, rows, start, wide = pieces[piece]
            kind = index % 4
            if kind >= 2:
                wide = wide // 2
                start += (kind - 2) * wide
            part = cp[f].at[rows_of(origin, top, rows), pl.ds(start, wide)]
            return pltpu.make_async_remote_copy(
                src_ref=part, dst_ref=part, send_sem=col_s.at[piece, index], recv_sem=col_r.at[piece, index],
                device_id=(dp, peer), device_id_type=MESH)

        def place(piece, d1, d2):
            return plane(piece % 2 == 0, d1, d2)

        def col_out(p):
            for index, d in ((0, 1), (1, -1)):
                send(column(p, index, tile, place(p, d, 0)))
            for index, d in ((4, 1), (5, -1)):
                send(column(p, index, tile, place(p, 0, d)))

        def col_near(p):
            for index, d in ((0, 1), (1, -1)):
                origin = place(p, -d, 0)
                column(p, index, origin, tile).wait_recv()
                send(column(p, 2 + index, origin, place(p, d, 0)))
            for b, d in ((1, 1), (3, -1)):
                origin = place(p, -d, 0)
                send(column(p, 4 + 4 * b, origin, place(p, 0, 1)))
                send(column(p, 5 + 4 * b, origin, place(p, 0, -1)))

        def col_far(p):
            origin = place(p, 2, 0)
            for index in (2, 3):
                column(p, index, origin, tile).wait_recv()
            send(column(p, 12, origin, place(p, 0, 1)))
            send(column(p, 13, origin, place(p, 0, -1)))

        def col_pass(p, b):
            for index, d in ((0, 1), (1, -1)):
                origin = place(p, -b, -d)
                column(p, 4 + 4 * b + index, origin, tile).wait_recv()
                send(column(p, 6 + 4 * b + index, origin, place(p, 0, d)))

        def col_end(p):
            for b in range(SIDE):
                for index in (2, 3):
                    column(p, 4 + 4 * b + index, place(p, -b, 2), tile).wait_recv()

        def multiply(f, start, wide, first, last):
            ks = pl.ds(start, wide)

            def step(n, _):
                cols = pl.ds(pl.multiple_of(n * WIDE, WIDE), WIDE)
                gram = lax.dot_general(rp[f][:, ks], cp[f][cols, ks], (((1,), (1,)), ((), ())),
                                       preferred_element_type=jnp.float32)
                if start > 0:
                    gram = outs[f][:, cols] + gram
                if start + wide == tokens:
                    gram = gram * (1.0 / tokens)
                outs[f][:, cols] = gram
                return 0

            lax.fori_loop(first, last, step, 0)

        def each(act, pair, *more):
            for p in pairs[pair]:
                act(p, *more)

        lax.fori_loop(0, units // 128, make_hidden, 0)
        pl.semaphore_wait(barrier, len(peers))
        start_swap(0)
        build_perm()
        end_swap(0)
        start_swap(1)
        for p in pairs[0]:
            pack(p)
            col_out(p)
        lax.fori_loop(0, units // 128, make_dgate, 0)
        end_swap(1)
        start_swap(2)
        each(pack, 1)
        each(col_near, 0)
        each(col_out, 1)
        each(col_pass, 0, 0)
        each(col_far, 0)
        end_swap(2)
        row_out(0)
        each(col_pass, 0, 1)
        each(col_pass, 0, 3)
        each(pack, 2)
        each(pack, 3)
        each(pack, 4)
        each(col_pass, 0, 2)
        each(col_near, 1)
        each(col_out, 2)
        row_pass(0)
        each(col_pass, 1, 0)
        each(col_far, 1)
        each(col_pass, 1, 1)
        row_far(0)
        row_out(1)
        each(col_pass, 1, 3)
        each(col_pass, 1, 2)
        row_end(0)
        each(col_near, 2)
        each(col_out, 3)
        each(col_end, 0)
        each(col_end, 1)
        multiply(0, 0, tokens, 0, 2)
        row_pass(1)
        each(col_pass, 2, 0)
        each(col_far, 2)
        multiply(0, 0, tokens, 2, 4)
        each(col_pass, 2, 1)
        each(col_pass, 2, 3)
        multiply(0, 0, tokens, 4, 5)
        row_far(1)
        each(col_pass, 2, 2)
        each(col_near, 3)
        each(col_out, 4)
        multiply(0, 0, tokens, 5, 7)
        row_end(1)
        each(col_pass, 3, 0)
        each(col_far, 3)
        each(col_end, 2)
        each(col_pass, 3, 1)
        each(col_pass, 3, 3)
        multiply(1, 0, 2 * F1_WIDTHS[0], 0, 4)
        each(col_pass, 3, 2)
        each(col_near, 4)
        multiply(1, 0, 2 * F1_WIDTHS[0], 4, 7)
        each(col_pass, 4, 0)
        each(col_far, 4)
        each(col_pass, 4, 1)
        each(col_pass, 4, 3)
        each(col_pass, 4, 2)
        each(col_end, 3)
        multiply(1, 2 * F1_WIDTHS[0], 2 * F1_WIDTHS[1], 0, 7)
        each(col_end, 4)
        for copy in sent:
            copy.wait_send()

    vmem = pltpu.VMEM
    outputs = [
        vmem((units, columns), jnp.float32),
        vmem((units, columns), jnp.float32),
        vmem((units, tokens), jnp.bfloat16),
        vmem((columns, tokens), jnp.bfloat16),
    ]
    scratch = [
        vmem((2, units, capacity), jnp.bfloat16),
        vmem((2, shards, group, capacity), jnp.bfloat16),
        vmem((len(slots), capacity, WIDE), jnp.bfloat16),
        vmem((units, tokens), jnp.bfloat16),
        vmem((columns, tokens), jnp.bfloat16),
        pltpu.SemaphoreType.DMA((len(parts), shards)),
        pltpu.SemaphoreType.DMA((len(parts), shards)),
        pltpu.SemaphoreType.DMA((len(parts),)),
        pltpu.SemaphoreType.DMA((2, 8)),
        pltpu.SemaphoreType.DMA((2, 8)),
        pltpu.SemaphoreType.DMA((len(pieces), 20)),
        pltpu.SemaphoreType.DMA((len(pieces), 20)),
    ]
    return kernel, outputs, scratch


def make_finish(units, columns, tokens):
    last = 2 * F1_WIDTHS[-1]

    def finish(act_in, grad_in, rp, cp, act_ref, grad_ref, total, act_s, grad_s):
        act_out = pltpu.make_async_copy(act_in, act_ref.at[:, 0, :], act_s)
        act_out.start()

        def copy(n):
            cols = pl.ds(pl.multiple_of(n * WIDE, WIDE), WIDE)
            return pltpu.make_async_copy(total.at[:, cols], grad_ref.at[:, 0, cols], grad_s.at[n])

        def step(n, _):
            cols = pl.ds(pl.multiple_of(n * WIDE, WIDE), WIDE)
            ks = pl.ds(tokens - last, last)
            gram = lax.dot_general(rp[:, ks], cp[cols, ks], (((1,), (1,)), ((), ())),
                                   preferred_element_type=jnp.float32)
            total[:, cols] = (grad_in[:, cols] + gram) * (1.0 / tokens)
            copy(n).start()
            return 0

        def wait(n, _):
            copy(n).wait()
            return 0

        lax.fori_loop(0, columns // WIDE, step, 0)
        lax.fori_loop(0, columns // WIDE, wait, 0)
        act_out.wait()

    scratch = [
        pltpu.VMEM((units, columns), jnp.float32),
        pltpu.SemaphoreType.DMA,
        pltpu.SemaphoreType.DMA((columns // WIDE,)),
    ]
    return finish, scratch


def solution(mesh):
    shards, tiles = mesh.shape["dp"], mesh.shape["tile"]

    def on_device(gate_pre, up_pre, grad_hidden, doc_tokens, doc_shard):
        capacity, units = gate_pre.shape
        group = units // shards
        columns = tiles * group
        kernel, outputs, scratch = make_kernel(capacity, units, group, shards, tiles)
        smem, vmem = pl.BlockSpec(memory_space=pltpu.SMEM), pl.BlockSpec(memory_space=pltpu.VMEM)
        panels = pl.pallas_call(
            kernel,
            out_shape=outputs,
            in_specs=[smem, smem, vmem, vmem, vmem],
            out_specs=[vmem] * len(outputs),
            scratch_shapes=scratch,
            compiler_params=pltpu.CompilerParams(
                collective_id=0, has_side_effects=True, vmem_limit_bytes=30 << 20),
            name="gram_exchange",
        )(doc_tokens, doc_shard, gate_pre, up_pre, grad_hidden)
        finish, scratch = make_finish(units, columns, TOK_DEV * shards)
        anywhere = pl.BlockSpec(memory_space=pl.ANY)
        act, grad = pl.pallas_call(
            finish,
            out_shape=[jax.ShapeDtypeStruct((units, 1, columns), jnp.float32)] * 2,
            in_specs=[vmem] * len(outputs),
            out_specs=[anywhere] * 2,
            scratch_shapes=scratch,
            compiler_params=pltpu.CompilerParams(vmem_limit_bytes=16 << 20),
            name="gram_finish",
        )(*panels)
        return act, grad

    return jax.shard_map(
        on_device,
        mesh=mesh,
        in_specs=(P("dp", "tile"), P("dp", "tile"), P("dp", "tile"), P(), P()),
        out_specs=(P("tile", "dp", None), P("tile", "dp", None)),
        check_vma=False,
    )
```

```python
import jax
import jax.numpy as jnp
from jax import lax
from jax.experimental import pallas as pl
from jax.experimental.pallas import tpu as pltpu
from jax.sharding import PartitionSpec as P

MESH = pl.DeviceIdType.MESH
TOK_DEV = 256
DOCS_SHARD = 4
F1_WIDTHS = (512, 256, 256)
WIDE = 256
SIDE = 4


def packing_blocks(shards, capacity, tokens):
    blocks = [[] for _ in range(tokens // WIDE)]
    for shard in range(shards):
        after = shards - shard
        first = max(DOCS_SHARD * shard, tokens - capacity * after)
        last = min(capacity * shard, tokens - DOCS_SHARD * after) + capacity
        for block in range(first // WIDE, -(-min(last, tokens) // WIDE)):
            blocks[block].append(shard)
    return blocks


def make_kernel(capacity, units, group, shards, tiles):
    tokens = TOK_DEV * shards
    blocks = packing_blocks(shards, capacity, tokens)
    slots = {}
    for n, members in enumerate(blocks):
        for shard in members:
            slots[n, shard] = len(slots)
    half = tokens // 2
    cut = group * 2 // 7
    parts = [(0, 0, cut), (0, cut, group - cut), (1, 0, group)]
    pieces = []
    for f, top, rows in parts[:2]:
        pieces += [(f, top, rows, 0, half), (f, top, rows, half, half)]
    start = 0
    for wide in F1_WIDTHS:
        pieces += [(1, 0, group, start, wide), (1, 0, group, start + wide, wide)]
        start += 2 * wide
    pairs = [(i, i + 1) for i in range(0, len(pieces), 2)]
    columns = tiles * group

    def kernel(tok_ref, own_ref, gate_hbm, up_hbm, down_hbm, act_ref, grad_ref, rp1, cp1,
               gate_ref, up_ref, down_ref, xt, rv, perm, rp0, cp0, load_s,
               swap_s, swap_r, local_s, row_s, row_r, col_s, col_r):
        outs, rp, cp = (act_ref, grad_ref), (rp0, rp1), (cp0, cp1)

        def send(copy):
            copy.start()

        loads_in = [pltpu.make_async_copy(source, target, load_s.at[i]) for i, (source, target) in enumerate(
            ((gate_hbm, gate_ref), (up_hbm, up_ref), (down_hbm, down_ref)))]
        for copy in loads_in:
            copy.start()

        dp, tile = lax.axis_index("dp"), lax.axis_index("tile")
        y, core = dp // 2, lax.rem(dp, 2)
        z, x = tile // SIDE, lax.rem(tile, SIDE)

        def plus(a, d):
            return lax.rem(a + d + SIDE, SIDE)

        def over_dp(offset):
            return lax.rem(dp + offset + shards, shards)

        def y_peer(d):
            return (plus(y, d) * 2 + core, tile)

        sibling = (y * 2 + 1 - core, tile)

        def plane(first_is_x, d1, d2):
            dx, dz = (d1, d2) if first_is_x else (d2, d1)
            return plus(z, dz) * SIDE + plus(x, dx)

        barrier = pltpu.get_barrier_semaphore()
        peers = [(over_dp(o), tile) for o in range(1, shards)]
        peers += [(dp, plane(True, d, 0)) for d in (1, 2, 3)] + [(dp, plane(True, 0, d)) for d in (1, 2, 3)]
        for peer in peers:
            pl.semaphore_signal(barrier, inc=1, device_id=peer, device_id_type=MESH)

        def count(i, loads):
            return tuple(v + jnp.where(own_ref[i] == j, tok_ref[i], 0) for j, v in enumerate(loads))

        loads = lax.fori_loop(0, shards * DOCS_SHARD, count, (jnp.int32(0),) * shards)
        own_load, offsets, total = jnp.int32(0), [], jnp.int32(0)
        for j in range(shards):
            own_load = own_load + jnp.where(dp == j, loads[j], 0)
            offsets.append(total)
            total = total + loads[j]

        live = lax.broadcasted_iota(jnp.int32, (capacity, 128), 0) < own_load

        def make_hidden(b, _):
            cols = pl.ds(pl.multiple_of(b * 128, 128), 128)
            g = gate_ref[:, cols].astype(jnp.float32)
            u = up_ref[:, cols].astype(jnp.float32)
            h = jnp.where(live, g * jax.nn.sigmoid(g) * u, 0.0)
            xt[0, cols, :] = h.T.astype(jnp.bfloat16)
            return 0

        def make_dgate(b, _):
            cols = pl.ds(pl.multiple_of(b * 128, 128), 128)
            g = gate_ref[:, cols].astype(jnp.float32)
            u = up_ref[:, cols].astype(jnp.float32)
            d = down_ref[:, cols].astype(jnp.float32)
            s = jax.nn.sigmoid(g)
            h = jnp.where(live, d * u * s * (1.0 + g * (1.0 - s)), 0.0)
            xt[1, cols, :] = h.T.astype(jnp.bfloat16)
            return 0

        def at_group(index):
            return pl.ds(pl.multiple_of(index * group, 16), group)

        def rows_of(index, top, rows):
            return pl.ds(pl.multiple_of(index * group + top, 16), rows)

        def swap(part, o):
            f, top, rows = parts[part]
            return pltpu.make_async_remote_copy(
                src_ref=xt.at[f, rows_of(over_dp(o), top, rows)], dst_ref=rv.at[f, dp, pl.ds(top, rows)],
                send_sem=swap_s.at[part], recv_sem=swap_r.at[part],
                device_id=(over_dp(o), tile), device_id_type=MESH)

        def swap_all(part):
            f, top, rows = parts[part]
            both = rv.at[f, pl.ds(0, shards - 1), pl.ds(top, rows)]
            return pltpu.make_async_remote_copy(
                src_ref=both, dst_ref=both, send_sem=swap_s.at[part], recv_sem=swap_r.at[part],
                device_id=(over_dp(1), tile), device_id_type=MESH)

        def swap_own(part):
            f, top, rows = parts[part]
            return pltpu.make_async_copy(
                xt.at[f, rows_of(dp, top, rows)], rv.at[f, dp, pl.ds(top, rows)], local_s.at[part])

        def start_swap(part):
            for o in (3, 4, 5, 2, 6, 7, 1):
                swap(part, o).start()
            swap_own(part).start()

        def end_swap(part):
            swap_own(part).wait()
            swap_all(part).wait_recv()

        def build_perm():
            diff = (lax.broadcasted_iota(jnp.int32, (capacity, WIDE), 1)
                    - lax.broadcasted_iota(jnp.int32, (capacity, WIDE), 0))
            for (n, shard), slot in slots.items():
                hit = diff == offsets[shard] - n * WIDE
                perm[slot] = jnp.where(hit, 1.0, 0.0).astype(jnp.bfloat16)

        def pack(piece):
            f, top, rows, start, wide = pieces[piece]
            for n in range(start // WIDE, (start + wide) // WIDE):
                acc = None
                for shard in blocks[n]:
                    term = jnp.dot(rv[f, shard, top:top + rows], perm[slots[n, shard]],
                                   preferred_element_type=jnp.float32)
                    acc = term if acc is None else acc + term
                packed = acc.astype(jnp.bfloat16)
                cp[f][rows_of(tile, top, rows), n * WIDE:(n + 1) * WIDE] = packed
                rp[f][rows_of(dp, top, rows), n * WIDE:(n + 1) * WIDE] = packed

        def row(f, index, origin, peer):
            lanes = pl.ds((index - 2) * half, half) if index in (2, 3) else slice(None)
            part = rp[f].at[at_group(origin), lanes]
            return pltpu.make_async_remote_copy(
                src_ref=part, dst_ref=part, send_sem=row_s.at[f], recv_sem=row_r.at[f, index],
                device_id=peer, device_id_type=MESH)

        def same_core(d):
            return plus(y, d) * 2 + core

        def row_out(f):
            send(row(f, 0, dp, y_peer(1)))
            send(row(f, 1, dp, y_peer(-1)))
            send(row(f, 4, dp, sibling))

        def row_pass(f):
            for index, d in ((0, 1), (1, -1)):
                row(f, index, same_core(-d), sibling).wait_recv()
                send(row(f, 2 + index, same_core(-d), y_peer(d)))
                send(row(f, 5 + index, same_core(-d), sibling))

        def row_far(f):
            for index in (2, 3):
                row(f, index, same_core(2), sibling).wait_recv()
            send(row(f, 7, same_core(2), sibling))

        def row_sent(f):
            whole = rp[f].at[pl.ds(0, 7 * group)]
            pltpu.make_async_remote_copy(
                src_ref=whole, dst_ref=whole, send_sem=row_s.at[f], recv_sem=row_r.at[f, 0],
                device_id=sibling, device_id_type=MESH).wait_send()

        def row_end(f):
            for index, d in ((4, 0), (5, -1), (6, 1), (7, 2)):
                row(f, index, plus(y, d) * 2 + 1 - core, sibling).wait_recv()

        def arrival(index):
            kind, b = index % 4, index // 4
            if kind < 2:
                return 2 * b + kind
            return 10 if b == 0 else 11

        def column(piece, index, origin, peer):
            f, top, rows, start, wide = pieces[piece]
            kind = index % 4
            if kind >= 2:
                wide = wide // 2
                start += (kind - 2) * wide
            part = cp[f].at[rows_of(origin, top, rows), pl.ds(start, wide)]
            return pltpu.make_async_remote_copy(
                src_ref=part, dst_ref=part, send_sem=col_s.at[piece], recv_sem=col_r.at[piece, arrival(index)],
                device_id=(dp, peer), device_id_type=MESH)

        def column_all(piece, index, count):
            f, top, rows, start, wide = pieces[piece]
            part = cp[f].at[pl.ds(0, count * rows), pl.ds(start, wide)]
            return pltpu.make_async_remote_copy(
                src_ref=part, dst_ref=part, send_sem=col_s.at[piece], recv_sem=col_r.at[piece, arrival(index)],
                device_id=(dp, tile), device_id_type=MESH)

        def place(piece, d1, d2):
            return plane(piece % 2 == 0, d1, d2)

        def col_first(p):
            for index, d in ((0, 1), (1, -1)):
                send(column(p, index, tile, place(p, d, 0)))

        def col_second(p):
            for index, d in ((4, 1), (5, -1)):
                send(column(p, index, tile, place(p, 0, d)))

        def col_out(pair):
            each(col_first, pair)
            each(col_second, pair)

        def col_near(p):
            for index, d in ((0, 1), (1, -1)):
                origin = place(p, -d, 0)
                column(p, index, origin, tile).wait_recv()
                send(column(p, 2 + index, origin, place(p, d, 0)))
            for b, d in ((1, 1), (3, -1)):
                origin = place(p, -d, 0)
                send(column(p, 4 + 4 * b, origin, place(p, 0, 1)))
                send(column(p, 5 + 4 * b, origin, place(p, 0, -1)))

        def col_far(p):
            origin = place(p, 2, 0)
            column_all(p, 2, 1).wait_recv()
            send(column(p, 12, origin, place(p, 0, 1)))
            send(column(p, 13, origin, place(p, 0, -1)))

        def col_pass(p, b):
            for index, d in ((0, 1), (1, -1)):
                origin = place(p, -b, -d)
                column(p, 4 + 4 * b + index, origin, tile).wait_recv()
                send(column(p, 6 + 4 * b + index, origin, place(p, 0, d)))

        def col_end(p):
            column_all(p, 6, SIDE).wait_recv()

        def multiply(f, start, wide, first, last):
            ks = pl.ds(start, wide)

            def step(n, _):
                cols = pl.ds(pl.multiple_of(n * WIDE, WIDE), WIDE)
                gram = lax.dot_general(rp[f][:, ks], cp[f][cols, ks], (((1,), (1,)), ((), ())),
                                       preferred_element_type=jnp.float32)
                if start > 0:
                    gram = outs[f][:, cols] + gram
                if start + wide == tokens:
                    gram = gram * (1.0 / tokens)
                outs[f][:, cols] = gram
                return 0

            lax.fori_loop(first, last, step, 0)

        def each(act, pair, *more):
            for p in pairs[pair]:
                act(p, *more)

        loads_in[0].wait()
        loads_in[1].wait()
        lax.fori_loop(0, units // 128, make_hidden, 0)
        pl.semaphore_wait(barrier, len(peers))
        start_swap(0)
        build_perm()
        loads_in[2].wait()
        lax.fori_loop(0, units // 128, make_dgate, 0)
        end_swap(0)
        start_swap(1)
        for p in pairs[0]:
            pack(p)
            col_first(p)
        each(col_second, 0)
        each(col_near, 0)
        end_swap(1)
        start_swap(2)
        for p in pairs[1]:
            pack(p)
            col_first(p)
        each(col_second, 1)
        each(col_pass, 0, 0)
        each(col_far, 0)
        each(col_pass, 0, 1)
        each(col_pass, 0, 3)
        each(col_near, 1)
        each(col_pass, 0, 2)
        end_swap(2)
        row_out(0)
        each(pack, 2)
        col_out(2)
        each(col_pass, 1, 0)
        each(col_far, 1)
        each(pack, 3)
        each(pack, 4)
        row_pass(0)
        each(col_pass, 1, 1)
        each(col_pass, 1, 3)
        each(col_near, 2)
        row_far(0)
        row_out(1)
        each(col_pass, 1, 2)
        col_out(3)
        row_end(0)
        each(col_pass, 2, 0)
        each(col_far, 2)
        each(col_end, 0)
        each(col_end, 1)
        multiply(0, 0, tokens, 0, 3)
        row_pass(1)
        each(col_pass, 2, 1)
        each(col_near, 3)
        each(col_pass, 2, 3)
        col_out(4)
        multiply(0, 0, tokens, 3, 5)
        row_far(1)
        each(col_pass, 2, 2)
        each(col_pass, 3, 0)
        each(col_far, 3)
        each(col_near, 4)
        multiply(0, 0, tokens, 5, 7)
        row_end(1)
        each(col_pass, 3, 1)
        each(col_pass, 3, 3)
        each(col_pass, 4, 0)
        each(col_far, 4)
        each(col_end, 2)
        multiply(1, 0, 2 * F1_WIDTHS[0], 0, 3)
        each(col_pass, 3, 2)
        each(col_pass, 4, 1)
        each(col_pass, 4, 3)
        multiply(1, 0, 2 * F1_WIDTHS[0], 3, 7)
        each(col_pass, 4, 2)
        each(col_end, 3)
        multiply(1, 2 * F1_WIDTHS[0], 2 * F1_WIDTHS[1], 0, 7)
        each(col_end, 4)
        for part in range(len(parts)):
            swap_all(part).wait_send()
        for f in range(2):
            row_sent(f)
        for p in range(len(pieces)):
            column_all(p, 0, 15).wait_send()

    vmem = pltpu.VMEM
    outputs = [
        vmem((units, columns), jnp.float32),
        vmem((units, columns), jnp.float32),
        vmem((units, tokens), jnp.bfloat16),
        vmem((columns, tokens), jnp.bfloat16),
    ]
    scratch = [vmem((capacity, units), jnp.bfloat16)] * 3 + [
        vmem((2, units, capacity), jnp.bfloat16),
        vmem((2, shards, group, capacity), jnp.bfloat16),
        vmem((len(slots), capacity, WIDE), jnp.bfloat16),
        vmem((units, tokens), jnp.bfloat16),
        vmem((columns, tokens), jnp.bfloat16),
        pltpu.SemaphoreType.DMA((3,)),
        pltpu.SemaphoreType.DMA((len(parts),)),
        pltpu.SemaphoreType.DMA((len(parts),)),
        pltpu.SemaphoreType.DMA((len(parts),)),
        pltpu.SemaphoreType.DMA((2,)),
        pltpu.SemaphoreType.DMA((2, 8)),
        pltpu.SemaphoreType.DMA((len(pieces),)),
        pltpu.SemaphoreType.DMA((len(pieces), 12)),
    ]
    return kernel, outputs, scratch


def make_finish(units, columns, tokens):
    last = 2 * F1_WIDTHS[-1]

    def finish(act_in, grad_in, rp, cp, act_ref, grad_ref, total, act_s, grad_s):
        act_out = pltpu.make_async_copy(act_in, act_ref.at[:, 0, :], act_s)
        act_out.start()

        def copy(n):
            cols = pl.ds(pl.multiple_of(n * WIDE, WIDE), WIDE)
            return pltpu.make_async_copy(total.at[:, cols], grad_ref.at[:, 0, cols], grad_s.at[n])

        def step(n, _):
            cols = pl.ds(pl.multiple_of(n * WIDE, WIDE), WIDE)
            ks = pl.ds(tokens - last, last)
            gram = lax.dot_general(rp[:, ks], cp[cols, ks], (((1,), (1,)), ((), ())),
                                   preferred_element_type=jnp.float32)
            total[:, cols] = (grad_in[:, cols] + gram) * (1.0 / tokens)
            copy(n).start()
            return 0

        def wait(n, _):
            copy(n).wait()
            return 0

        lax.fori_loop(0, columns // WIDE, step, 0)
        lax.fori_loop(0, columns // WIDE, wait, 0)
        act_out.wait()

    scratch = [
        pltpu.VMEM((units, columns), jnp.float32),
        pltpu.SemaphoreType.DMA,
        pltpu.SemaphoreType.DMA((columns // WIDE,)),
    ]
    return finish, scratch


def solution(mesh):
    shards, tiles = mesh.shape["dp"], mesh.shape["tile"]

    def on_device(gate_pre, up_pre, grad_hidden, doc_tokens, doc_shard):
        capacity, units = gate_pre.shape
        group = units // shards
        columns = tiles * group
        kernel, outputs, scratch = make_kernel(capacity, units, group, shards, tiles)
        smem, vmem = pl.BlockSpec(memory_space=pltpu.SMEM), pl.BlockSpec(memory_space=pltpu.VMEM)
        hbm = pl.BlockSpec(memory_space=pltpu.HBM)
        panels = pl.pallas_call(
            kernel,
            out_shape=outputs,
            in_specs=[smem, smem, hbm, hbm, hbm],
            out_specs=[vmem] * len(outputs),
            scratch_shapes=scratch,
            compiler_params=pltpu.CompilerParams(
                collective_id=0, has_side_effects=True, vmem_limit_bytes=30 << 20),
            name="gram_exchange",
        )(*(pltpu.with_memory_space_constraint(v, pltpu.HBM)
            for v in (doc_tokens, doc_shard, gate_pre, up_pre, grad_hidden)))
        finish, scratch = make_finish(units, columns, TOK_DEV * shards)
        anywhere = pl.BlockSpec(memory_space=pl.ANY)
        act, grad = pl.pallas_call(
            finish,
            out_shape=[jax.ShapeDtypeStruct((units, 1, columns), jnp.float32)] * 2,
            in_specs=[vmem] * len(outputs),
            out_specs=[anywhere] * 2,
            scratch_shapes=scratch,
            compiler_params=pltpu.CompilerParams(vmem_limit_bytes=16 << 20),
            name="gram_finish",
        )(*panels)
        return act, grad

    return jax.shard_map(
        on_device,
        mesh=mesh,
        in_specs=(P("dp", "tile"), P("dp", "tile"), P("dp", "tile"), P(), P()),
        out_specs=(P("tile", "dp", None), P("tile", "dp", None)),
        check_vma=False,
    )
```

```python
import jax
import jax.numpy as jnp
from jax import lax
from jax.experimental import pallas as pl
from jax.experimental.pallas import tpu as pltpu
from jax.sharding import PartitionSpec as P

MESH = pl.DeviceIdType.MESH
TOK_DEV = 256
DOCS_SHARD = 4
F1_WIDTHS = (512, 256, 256)
WIDE = 256
SIDE = 4


def packing_blocks(shards, capacity, tokens):
    blocks = [[] for _ in range(tokens // WIDE)]
    for shard in range(shards):
        after = shards - shard
        first = max(DOCS_SHARD * shard, tokens - capacity * after)
        last = min(capacity * shard, tokens - DOCS_SHARD * after) + capacity
        for block in range(first // WIDE, -(-min(last, tokens) // WIDE)):
            blocks[block].append(shard)
    return blocks


def make_kernel(capacity, units, group, shards, tiles):
    tokens = TOK_DEV * shards
    blocks = packing_blocks(shards, capacity, tokens)
    slots = {}
    for n, members in enumerate(blocks):
        for shard in members:
            slots[n, shard] = len(slots)
    half = tokens // 2
    cut = group * 2 // 7
    parts = [(0, 0, cut), (0, cut, group - cut), (1, 0, group)]
    pieces = []
    for f, top, rows in parts[:2]:
        pieces += [(f, top, rows, 0, half), (f, top, rows, half, half)]
    start = 0
    for wide in F1_WIDTHS:
        pieces += [(1, 0, group, start, wide), (1, 0, group, start + wide, wide)]
        start += 2 * wide
    pairs = [(i, i + 1) for i in range(0, len(pieces), 2)]
    columns = tiles * group

    def kernel(tok_ref, own_ref, gate_hbm, up_hbm, down_hbm, act_ref, grad_ref, rp1, cp1,
               gate_ref, up_ref, down_ref, xt, rv, perm, rp0, cp0, load_s,
               swap_s, swap_r, local_s, row_s, row_r, col_s, col_r):
        outs, rp, cp = (act_ref, grad_ref), (rp0, rp1), (cp0, cp1)

        def send(copy):
            copy.start()

        def fetch(i, b):
            cols = pl.ds(pl.multiple_of(b * 128, 128), 128)
            source = (gate_hbm, up_hbm, down_hbm)[i]
            target = (gate_ref, up_ref, down_ref)[i]
            return pltpu.make_async_copy(source.at[:, cols], target.at[:, cols], load_s.at[i, b])

        def fetch_pair(b, _):
            fetch(0, b).start()
            fetch(1, b).start()
            return 0

        def fetch_down(b, _):
            fetch(2, b).start()
            return 0

        lax.fori_loop(0, units // 128, fetch_pair, 0)
        lax.fori_loop(0, units // 128, fetch_down, 0)

        dp, tile = lax.axis_index("dp"), lax.axis_index("tile")
        y, core = dp // 2, lax.rem(dp, 2)
        z, x = tile // SIDE, lax.rem(tile, SIDE)

        def plus(a, d):
            return lax.rem(a + d + SIDE, SIDE)

        def over_dp(offset):
            return lax.rem(dp + offset + shards, shards)

        def y_peer(d):
            return (plus(y, d) * 2 + core, tile)

        sibling = (y * 2 + 1 - core, tile)

        def plane(first_is_x, d1, d2):
            dx, dz = (d1, d2) if first_is_x else (d2, d1)
            return plus(z, dz) * SIDE + plus(x, dx)

        barrier = pltpu.get_barrier_semaphore()
        peers = [(over_dp(o), tile) for o in range(1, shards)]
        peers += [(dp, plane(True, d, 0)) for d in (1, 2, 3)] + [(dp, plane(True, 0, d)) for d in (1, 2, 3)]
        for peer in peers:
            pl.semaphore_signal(barrier, inc=1, device_id=peer, device_id_type=MESH)

        def count(i, loads):
            return tuple(v + jnp.where(own_ref[i] == j, tok_ref[i], 0) for j, v in enumerate(loads))

        loads = lax.fori_loop(0, shards * DOCS_SHARD, count, (jnp.int32(0),) * shards)
        own_load, offsets, total = jnp.int32(0), [], jnp.int32(0)
        for j in range(shards):
            own_load = own_load + jnp.where(dp == j, loads[j], 0)
            offsets.append(total)
            total = total + loads[j]

        live = lax.broadcasted_iota(jnp.int32, (capacity, 128), 0) < own_load

        def make_hidden(b, _):
            fetch(0, b).wait()
            fetch(1, b).wait()
            cols = pl.ds(pl.multiple_of(b * 128, 128), 128)
            g = gate_ref[:, cols].astype(jnp.float32)
            u = up_ref[:, cols].astype(jnp.float32)
            h = jnp.where(live, g * jax.nn.sigmoid(g) * u, 0.0)
            xt[0, cols, :] = h.T.astype(jnp.bfloat16)
            return 0

        def make_dgate(b, _):
            fetch(2, b).wait()
            cols = pl.ds(pl.multiple_of(b * 128, 128), 128)
            g = gate_ref[:, cols].astype(jnp.float32)
            u = up_ref[:, cols].astype(jnp.float32)
            d = down_ref[:, cols].astype(jnp.float32)
            s = jax.nn.sigmoid(g)
            h = jnp.where(live, d * u * s * (1.0 + g * (1.0 - s)), 0.0)
            xt[1, cols, :] = h.T.astype(jnp.bfloat16)
            return 0

        def at_group(index):
            return pl.ds(pl.multiple_of(index * group, 16), group)

        def rows_of(index, top, rows):
            return pl.ds(pl.multiple_of(index * group + top, 16), rows)

        def swap(part, o):
            f, top, rows = parts[part]
            return pltpu.make_async_remote_copy(
                src_ref=xt.at[f, rows_of(over_dp(o), top, rows)], dst_ref=rv.at[f, dp, pl.ds(top, rows)],
                send_sem=swap_s.at[part], recv_sem=swap_r.at[part],
                device_id=(over_dp(o), tile), device_id_type=MESH)

        def swap_all(part):
            f, top, rows = parts[part]
            both = rv.at[f, pl.ds(0, shards - 1), pl.ds(top, rows)]
            return pltpu.make_async_remote_copy(
                src_ref=both, dst_ref=both, send_sem=swap_s.at[part], recv_sem=swap_r.at[part],
                device_id=(over_dp(1), tile), device_id_type=MESH)

        def swap_own(part):
            f, top, rows = parts[part]
            return pltpu.make_async_copy(
                xt.at[f, rows_of(dp, top, rows)], rv.at[f, dp, pl.ds(top, rows)], local_s.at[part])

        def start_swap(part):
            for o in (3, 4, 5, 2, 6, 7, 1):
                swap(part, o).start()
            swap_own(part).start()

        def end_swap(part):
            swap_own(part).wait()
            swap_all(part).wait_recv()

        def build_perm():
            diff = (lax.broadcasted_iota(jnp.int32, (capacity, WIDE), 1)
                    - lax.broadcasted_iota(jnp.int32, (capacity, WIDE), 0))
            for (n, shard), slot in slots.items():
                hit = diff == offsets[shard] - n * WIDE
                perm[slot] = jnp.where(hit, 1.0, 0.0).astype(jnp.bfloat16)

        def pack(piece):
            f, top, rows, start, wide = pieces[piece]
            for n in range(start // WIDE, (start + wide) // WIDE):
                acc = None
                for shard in blocks[n]:
                    term = jnp.dot(rv[f, shard, top:top + rows], perm[slots[n, shard]],
                                   preferred_element_type=jnp.float32)
                    acc = term if acc is None else acc + term
                packed = acc.astype(jnp.bfloat16)
                cp[f][rows_of(tile, top, rows), n * WIDE:(n + 1) * WIDE] = packed
                rp[f][rows_of(dp, top, rows), n * WIDE:(n + 1) * WIDE] = packed

        def row(f, index, origin, peer):
            lanes = pl.ds((index - 2) * half, half) if index in (2, 3) else slice(None)
            part = rp[f].at[at_group(origin), lanes]
            return pltpu.make_async_remote_copy(
                src_ref=part, dst_ref=part, send_sem=row_s.at[f], recv_sem=row_r.at[f, index],
                device_id=peer, device_id_type=MESH)

        def same_core(d):
            return plus(y, d) * 2 + core

        def row_out(f):
            send(row(f, 0, dp, y_peer(1)))
            send(row(f, 1, dp, y_peer(-1)))
            send(row(f, 4, dp, sibling))

        def row_pass(f):
            for index, d in ((0, 1), (1, -1)):
                row(f, index, same_core(-d), sibling).wait_recv()
                send(row(f, 2 + index, same_core(-d), y_peer(d)))
                send(row(f, 5 + index, same_core(-d), sibling))

        def row_far(f):
            for index in (2, 3):
                row(f, index, same_core(2), sibling).wait_recv()
            send(row(f, 7, same_core(2), sibling))

        def row_sent(f):
            whole = rp[f].at[pl.ds(0, 7 * group)]
            pltpu.make_async_remote_copy(
                src_ref=whole, dst_ref=whole, send_sem=row_s.at[f], recv_sem=row_r.at[f, 0],
                device_id=sibling, device_id_type=MESH).wait_send()

        def row_end(f):
            for index, d in ((4, 0), (5, -1), (6, 1), (7, 2)):
                row(f, index, plus(y, d) * 2 + 1 - core, sibling).wait_recv()

        def arrival(index):
            kind, b = index % 4, index // 4
            if kind < 2:
                return 2 * b + kind
            return 10 if b == 0 else 11

        def column(piece, index, origin, peer):
            f, top, rows, start, wide = pieces[piece]
            kind = index % 4
            if kind >= 2:
                wide = wide // 2
                start += (kind - 2) * wide
            part = cp[f].at[rows_of(origin, top, rows), pl.ds(start, wide)]
            return pltpu.make_async_remote_copy(
                src_ref=part, dst_ref=part, send_sem=col_s.at[piece], recv_sem=col_r.at[piece, arrival(index)],
                device_id=(dp, peer), device_id_type=MESH)

        def column_all(piece, index, count):
            f, top, rows, start, wide = pieces[piece]
            part = cp[f].at[pl.ds(0, count * rows), pl.ds(start, wide)]
            return pltpu.make_async_remote_copy(
                src_ref=part, dst_ref=part, send_sem=col_s.at[piece], recv_sem=col_r.at[piece, arrival(index)],
                device_id=(dp, tile), device_id_type=MESH)

        def place(piece, d1, d2):
            return plane(piece % 2 == 0, d1, d2)

        def col_first(p):
            for index, d in ((0, 1), (1, -1)):
                send(column(p, index, tile, place(p, d, 0)))

        def col_second(p):
            for index, d in ((4, 1), (5, -1)):
                send(column(p, index, tile, place(p, 0, d)))

        def col_out(pair):
            each(col_first, pair)
            each(col_second, pair)

        def col_near(p):
            for index, d in ((0, 1), (1, -1)):
                origin = place(p, -d, 0)
                column(p, index, origin, tile).wait_recv()
                send(column(p, 2 + index, origin, place(p, d, 0)))
            for b, d in ((1, 1), (3, -1)):
                origin = place(p, -d, 0)
                send(column(p, 4 + 4 * b, origin, place(p, 0, 1)))
                send(column(p, 5 + 4 * b, origin, place(p, 0, -1)))

        def col_far(p):
            origin = place(p, 2, 0)
            column_all(p, 2, 1).wait_recv()
            send(column(p, 12, origin, place(p, 0, 1)))
            send(column(p, 13, origin, place(p, 0, -1)))

        def col_pass(p, b):
            for index, d in ((0, 1), (1, -1)):
                origin = place(p, -b, -d)
                column(p, 4 + 4 * b + index, origin, tile).wait_recv()
                send(column(p, 6 + 4 * b + index, origin, place(p, 0, d)))

        def col_end(p):
            column_all(p, 6, SIDE).wait_recv()

        def multiply(f, start, wide, first, last):
            ks = pl.ds(start, wide)

            def step(i, _):
                part = pl.ds(pl.multiple_of(i * (units // 2), 16), units // 2)
                gram = lax.dot_general(rp[f][part, ks], cp[f][:, ks], (((1,), (1,)), ((), ())),
                                       preferred_element_type=jnp.float32)
                if start > 0:
                    gram = outs[f][part] + gram
                if start + wide == tokens:
                    gram = gram * (1.0 / tokens)
                outs[f][part] = gram
                return 0

            lax.fori_loop(first, last, step, 0)

        def each(act, pair, *more):
            for p in pairs[pair]:
                act(p, *more)

        lax.fori_loop(0, units // 128, make_hidden, 0)
        pl.semaphore_wait(barrier, len(peers))
        start_swap(0)
        build_perm()
        lax.fori_loop(0, units // 128, make_dgate, 0)
        end_swap(0)
        start_swap(1)
        for p in pairs[0]:
            pack(p)
            col_first(p)
        each(col_second, 0)
        each(col_near, 0)
        each(col_pass, 0, 0)
        end_swap(1)
        start_swap(2)
        for p in pairs[1]:
            pack(p)
            col_first(p)
        each(col_far, 0)
        each(col_second, 1)
        each(col_pass, 0, 1)
        each(col_near, 1)
        each(col_pass, 0, 3)
        each(col_pass, 0, 2)
        end_swap(2)
        row_out(0)
        for p in pairs[2]:
            pack(p)
            col_first(p)
        each(col_second, 2)
        each(col_pass, 1, 0)
        each(col_far, 1)
        each(pack, 3)
        each(pack, 4)
        each(col_near, 2)
        each(col_pass, 1, 1)
        row_pass(0)
        each(col_first, 3)
        each(col_pass, 1, 3)
        each(col_second, 3)
        each(col_pass, 1, 2)
        row_far(0)
        row_out(1)
        each(col_near, 3)
        row_end(0)
        each(col_pass, 2, 0)
        each(col_far, 2)
        each(col_first, 4)
        each(col_end, 0)
        each(col_end, 1)
        multiply(0, 0, tokens, 0, 1)
        each(col_pass, 2, 1)
        each(col_second, 4)
        row_pass(1)
        each(col_pass, 2, 3)
        each(col_near, 4)
        multiply(0, 0, tokens, 1, 2)
        each(col_far, 3)
        each(col_pass, 2, 2)
        row_far(1)
        each(col_pass, 3, 0)
        each(col_pass, 3, 1)
        each(col_far, 4)
        each(col_end, 2)
        row_end(1)
        each(col_pass, 3, 3)
        each(col_pass, 4, 0)
        each(col_pass, 3, 2)
        each(col_pass, 4, 1)
        each(col_pass, 4, 3)
        each(col_pass, 4, 2)
        multiply(1, 0, 2 * F1_WIDTHS[0], 0, 2)
        each(col_end, 3)
        each(col_end, 4)
        for part in range(len(parts)):
            swap_all(part).wait_send()
        for f in range(2):
            row_sent(f)
        for p in range(len(pieces)):
            column_all(p, 0, 15).wait_send()

    vmem = pltpu.VMEM
    outputs = [
        vmem((units, columns), jnp.float32),
        vmem((units, columns), jnp.float32),
        vmem((units, tokens), jnp.bfloat16),
        vmem((columns, tokens), jnp.bfloat16),
    ]
    scratch = [vmem((capacity, units), jnp.bfloat16)] * 3 + [
        vmem((2, units, capacity), jnp.bfloat16),
        vmem((2, shards, group, capacity), jnp.bfloat16),
        vmem((len(slots), capacity, WIDE), jnp.bfloat16),
        vmem((units, tokens), jnp.bfloat16),
        vmem((columns, tokens), jnp.bfloat16),
        pltpu.SemaphoreType.DMA((3, units // 128)),
        pltpu.SemaphoreType.DMA((len(parts),)),
        pltpu.SemaphoreType.DMA((len(parts),)),
        pltpu.SemaphoreType.DMA((len(parts),)),
        pltpu.SemaphoreType.DMA((2,)),
        pltpu.SemaphoreType.DMA((2, 8)),
        pltpu.SemaphoreType.DMA((len(pieces),)),
        pltpu.SemaphoreType.DMA((len(pieces), 12)),
    ]
    return kernel, outputs, scratch


def make_finish(units, columns, tokens):
    last = 2 * sum(F1_WIDTHS[1:])

    def finish(act_in, grad_in, rp, cp, act_ref, grad_ref, total, act_s, grad_s):
        act_out = pltpu.make_async_copy(act_in, act_ref.at[:, 0, :], act_s)
        act_out.start()

        def half(i):
            return pl.ds(pl.multiple_of(i * (units // 2), 16), units // 2)

        def copy(i):
            return pltpu.make_async_copy(total.at[half(i)], grad_ref.at[half(i), 0, :], grad_s.at[i])

        def step(i, _):
            ks = pl.ds(tokens - last, last)
            gram = lax.dot_general(rp[half(i), ks], cp[:, ks], (((1,), (1,)), ((), ())),
                                   preferred_element_type=jnp.float32)
            total[half(i)] = (grad_in[half(i)] + gram) * (1.0 / tokens)
            copy(i).start()
            return 0

        lax.fori_loop(0, 2, step, 0)
        for i in range(2):
            copy(i).wait()
        act_out.wait()

    scratch = [
        pltpu.VMEM((units, columns), jnp.float32),
        pltpu.SemaphoreType.DMA,
        pltpu.SemaphoreType.DMA((2,)),
    ]
    return finish, scratch


def solution(mesh):
    shards, tiles = mesh.shape["dp"], mesh.shape["tile"]

    def on_device(gate_pre, up_pre, grad_hidden, doc_tokens, doc_shard):
        capacity, units = gate_pre.shape
        group = units // shards
        columns = tiles * group
        kernel, outputs, scratch = make_kernel(capacity, units, group, shards, tiles)
        smem, vmem = pl.BlockSpec(memory_space=pltpu.SMEM), pl.BlockSpec(memory_space=pltpu.VMEM)
        hbm = pl.BlockSpec(memory_space=pltpu.HBM)
        panels = pl.pallas_call(
            kernel,
            out_shape=outputs,
            in_specs=[smem, smem, hbm, hbm, hbm],
            out_specs=[vmem] * len(outputs),
            scratch_shapes=scratch,
            compiler_params=pltpu.CompilerParams(
                collective_id=0, has_side_effects=True, vmem_limit_bytes=30 << 20),
            name="gram_exchange",
        )(*(pltpu.with_memory_space_constraint(v, pltpu.HBM)
            for v in (doc_tokens, doc_shard, gate_pre, up_pre, grad_hidden)))
        finish, scratch = make_finish(units, columns, TOK_DEV * shards)
        anywhere = pl.BlockSpec(memory_space=pl.ANY)
        act, grad = pl.pallas_call(
            finish,
            out_shape=[jax.ShapeDtypeStruct((units, 1, columns), jnp.float32)] * 2,
            in_specs=[vmem] * len(outputs),
            out_specs=[anywhere] * 2,
            scratch_shapes=scratch,
            compiler_params=pltpu.CompilerParams(vmem_limit_bytes=16 << 20),
            name="gram_finish",
        )(*panels)
        return act, grad

    return jax.shard_map(
        on_device,
        mesh=mesh,
        in_specs=(P("dp", "tile"), P("dp", "tile"), P("dp", "tile"), P(), P()),
        out_specs=(P("tile", "dp", None), P("tile", "dp", None)),
        check_vma=False,
    )
```

```python
import jax
import jax.numpy as jnp
from jax import lax
from jax.experimental import pallas as pl
from jax.experimental.pallas import tpu as pltpu
from jax.sharding import PartitionSpec as P

MESH = pl.DeviceIdType.MESH
TOK_DEV = 256
DOCS_SHARD = 4
F1_WIDTHS = (512, 512)
WIDE = 256
SIDE = 4


def packing_blocks(shards, capacity, tokens):
    blocks = [[] for _ in range(tokens // WIDE)]
    for shard in range(shards):
        after = shards - shard
        first = max(DOCS_SHARD * shard, tokens - capacity * after)
        last = min(capacity * shard, tokens - DOCS_SHARD * after) + capacity
        for block in range(first // WIDE, -(-min(last, tokens) // WIDE)):
            blocks[block].append(shard)
    return blocks


def make_kernel(capacity, units, group, shards, tiles):
    tokens = TOK_DEV * shards
    blocks = packing_blocks(shards, capacity, tokens)
    slots = {}
    for n, members in enumerate(blocks):
        for shard in members:
            slots[n, shard] = len(slots)
    half = tokens // 2
    cut = group * 2 // 7
    parts = [(0, 0, cut), (0, cut, group - cut), (1, 0, group)]
    pieces = []
    for f, top, rows in parts[:2]:
        pieces += [(f, top, rows, 0, half), (f, top, rows, half, half)]
    start = 0
    for wide in F1_WIDTHS:
        pieces += [(1, 0, group, start, wide), (1, 0, group, start + wide, wide)]
        start += 2 * wide
    pairs = [(i, i + 1) for i in range(0, len(pieces), 2)]
    columns = tiles * group

    def kernel(tok_ref, own_ref, gate_hbm, up_hbm, down_hbm, act_ref, grad_ref, rp1, cp1,
               gate_ref, up_ref, down_ref, xt, rv, perm, rp0, cp0, load_s,
               swap_s, swap_r, local_s, row_s, row_r, col_s, col_r):
        outs, rp, cp = (act_ref, grad_ref), (rp0, rp1), (cp0, cp1)

        def send(copy):
            copy.start()

        def fetch(i, b):
            cols = pl.ds(pl.multiple_of(b * 128, 128), 128)
            source = (gate_hbm, up_hbm, down_hbm)[i]
            target = (gate_ref, up_ref, down_ref)[i]
            return pltpu.make_async_copy(source.at[:, cols], target.at[:, cols], load_s.at[i, b])

        def fetch_pair(b, _):
            fetch(0, b).start()
            fetch(1, b).start()
            return 0

        def fetch_down(b, _):
            fetch(2, b).start()
            return 0

        lax.fori_loop(0, units // 128, fetch_pair, 0)
        lax.fori_loop(0, units // 128, fetch_down, 0)

        dp, tile = lax.axis_index("dp"), lax.axis_index("tile")
        y, core = dp // 2, lax.rem(dp, 2)
        z, x = tile // SIDE, lax.rem(tile, SIDE)

        def plus(a, d):
            return lax.rem(a + d + SIDE, SIDE)

        def over_dp(offset):
            return lax.rem(dp + offset + shards, shards)

        def y_peer(d):
            return (plus(y, d) * 2 + core, tile)

        sibling = (y * 2 + 1 - core, tile)

        def plane(first_is_x, d1, d2):
            dx, dz = (d1, d2) if first_is_x else (d2, d1)
            return plus(z, dz) * SIDE + plus(x, dx)

        barrier = pltpu.get_barrier_semaphore()
        peers = [(over_dp(o), tile) for o in range(1, shards)]
        peers += [(dp, plane(True, d, 0)) for d in (1, 2, 3)] + [(dp, plane(True, 0, d)) for d in (1, 2, 3)]
        for peer in peers:
            pl.semaphore_signal(barrier, inc=1, device_id=peer, device_id_type=MESH)

        def count(i, loads):
            return tuple(v + jnp.where(own_ref[i] == j, tok_ref[i], 0) for j, v in enumerate(loads))

        loads = lax.fori_loop(0, shards * DOCS_SHARD, count, (jnp.int32(0),) * shards)
        own_load, offsets, total = jnp.int32(0), [], jnp.int32(0)
        for j in range(shards):
            own_load = own_load + jnp.where(dp == j, loads[j], 0)
            offsets.append(total)
            total = total + loads[j]

        live = lax.broadcasted_iota(jnp.int32, (capacity, 128), 0) < own_load

        def make_hidden(b, _):
            fetch(0, b).wait()
            fetch(1, b).wait()
            cols = pl.ds(pl.multiple_of(b * 128, 128), 128)
            g = gate_ref[:, cols].astype(jnp.float32)
            u = up_ref[:, cols].astype(jnp.float32)
            h = jnp.where(live, g * jax.nn.sigmoid(g) * u, 0.0)
            xt[0, cols, :] = h.T.astype(jnp.bfloat16)
            return 0

        def make_dgate(b, _):
            fetch(2, b).wait()
            cols = pl.ds(pl.multiple_of(b * 128, 128), 128)
            g = gate_ref[:, cols].astype(jnp.float32)
            u = up_ref[:, cols].astype(jnp.float32)
            d = down_ref[:, cols].astype(jnp.float32)
            s = jax.nn.sigmoid(g)
            h = jnp.where(live, d * u * s * (1.0 + g * (1.0 - s)), 0.0)
            xt[1, cols, :] = h.T.astype(jnp.bfloat16)
            return 0

        def at_group(index):
            return pl.ds(pl.multiple_of(index * group, 16), group)

        def rows_of(index, top, rows):
            return pl.ds(pl.multiple_of(index * group + top, 16), rows)

        def swap(part, o):
            f, top, rows = parts[part]
            return pltpu.make_async_remote_copy(
                src_ref=xt.at[f, rows_of(over_dp(o), top, rows)], dst_ref=rv.at[f, dp, pl.ds(top, rows)],
                send_sem=swap_s.at[part], recv_sem=swap_r.at[part],
                device_id=(over_dp(o), tile), device_id_type=MESH)

        def swap_all(part):
            f, top, rows = parts[part]
            both = rv.at[f, pl.ds(0, shards - 1), pl.ds(top, rows)]
            return pltpu.make_async_remote_copy(
                src_ref=both, dst_ref=both, send_sem=swap_s.at[part], recv_sem=swap_r.at[part],
                device_id=(over_dp(1), tile), device_id_type=MESH)

        def swap_own(part):
            f, top, rows = parts[part]
            return pltpu.make_async_copy(
                xt.at[f, rows_of(dp, top, rows)], rv.at[f, dp, pl.ds(top, rows)], local_s.at[part])

        def start_swap(part):
            for o in (3, 4, 5, 2, 6, 7, 1):
                swap(part, o).start()
            swap_own(part).start()

        def end_swap(part):
            swap_own(part).wait()
            swap_all(part).wait_recv()

        def build_perm():
            diff = (lax.broadcasted_iota(jnp.int32, (capacity, WIDE), 1)
                    - lax.broadcasted_iota(jnp.int32, (capacity, WIDE), 0))
            for (n, shard), slot in slots.items():
                hit = diff == offsets[shard] - n * WIDE
                perm[slot] = jnp.where(hit, 1.0, 0.0).astype(jnp.bfloat16)

        def pack(piece):
            f, top, rows, start, wide = pieces[piece]
            for n in range(start // WIDE, (start + wide) // WIDE):
                acc = None
                for shard in blocks[n]:
                    term = jnp.dot(rv[f, shard, top:top + rows], perm[slots[n, shard]],
                                   preferred_element_type=jnp.float32)
                    acc = term if acc is None else acc + term
                packed = acc.astype(jnp.bfloat16)
                cp[f][rows_of(tile, top, rows), n * WIDE:(n + 1) * WIDE] = packed
                rp[f][rows_of(dp, top, rows), n * WIDE:(n + 1) * WIDE] = packed

        def row(f, index, origin, peer):
            lanes = pl.ds((index - 2) * half, half) if index in (2, 3) else slice(None)
            part = rp[f].at[at_group(origin), lanes]
            return pltpu.make_async_remote_copy(
                src_ref=part, dst_ref=part, send_sem=row_s.at[f], recv_sem=row_r.at[f, index],
                device_id=peer, device_id_type=MESH)

        def same_core(d):
            return plus(y, d) * 2 + core

        def row_out(f):
            send(row(f, 0, dp, y_peer(1)))
            send(row(f, 1, dp, y_peer(-1)))
            send(row(f, 4, dp, sibling))

        def row_pass(f):
            for index, d in ((0, 1), (1, -1)):
                row(f, index, same_core(-d), sibling).wait_recv()
                send(row(f, 2 + index, same_core(-d), y_peer(d)))
                send(row(f, 5 + index, same_core(-d), sibling))

        def row_far(f):
            for index in (2, 3):
                row(f, index, same_core(2), sibling).wait_recv()
            send(row(f, 7, same_core(2), sibling))

        def row_sent(f):
            whole = rp[f].at[pl.ds(0, 7 * group)]
            pltpu.make_async_remote_copy(
                src_ref=whole, dst_ref=whole, send_sem=row_s.at[f], recv_sem=row_r.at[f, 0],
                device_id=sibling, device_id_type=MESH).wait_send()

        def row_end(f):
            for index, d in ((4, 0), (5, -1), (6, 1), (7, 2)):
                row(f, index, plus(y, d) * 2 + 1 - core, sibling).wait_recv()

        def arrival(index):
            kind, b = index % 4, index // 4
            if kind < 2:
                return 2 * b + kind
            return 10 if b == 0 else 11

        def column(piece, index, origin, peer):
            f, top, rows, start, wide = pieces[piece]
            kind = index % 4
            if kind >= 2:
                wide = wide // 2
                start += (kind - 2) * wide
            part = cp[f].at[rows_of(origin, top, rows), pl.ds(start, wide)]
            return pltpu.make_async_remote_copy(
                src_ref=part, dst_ref=part, send_sem=col_s.at[piece], recv_sem=col_r.at[piece, arrival(index)],
                device_id=(dp, peer), device_id_type=MESH)

        def column_all(piece, index, count):
            f, top, rows, start, wide = pieces[piece]
            part = cp[f].at[pl.ds(0, count * rows), pl.ds(start, wide)]
            return pltpu.make_async_remote_copy(
                src_ref=part, dst_ref=part, send_sem=col_s.at[piece], recv_sem=col_r.at[piece, arrival(index)],
                device_id=(dp, tile), device_id_type=MESH)

        def place(piece, d1, d2):
            return plane(piece % 2 == 0, d1, d2)

        def col_first(p):
            for index, d in ((0, 1), (1, -1)):
                send(column(p, index, tile, place(p, d, 0)))

        def col_second(p):
            for index, d in ((4, 1), (5, -1)):
                send(column(p, index, tile, place(p, 0, d)))

        def col_out(pair):
            each(col_first, pair)
            each(col_second, pair)

        def col_near(p):
            for index, d in ((0, 1), (1, -1)):
                origin = place(p, -d, 0)
                column(p, index, origin, tile).wait_recv()
                send(column(p, 2 + index, origin, place(p, d, 0)))
            for b, d in ((1, 1), (3, -1)):
                origin = place(p, -d, 0)
                send(column(p, 4 + 4 * b, origin, place(p, 0, 1)))
                send(column(p, 5 + 4 * b, origin, place(p, 0, -1)))

        def col_far(p):
            origin = place(p, 2, 0)
            column_all(p, 2, 1).wait_recv()
            send(column(p, 12, origin, place(p, 0, 1)))
            send(column(p, 13, origin, place(p, 0, -1)))

        def col_pass(p, b):
            for index, d in ((0, 1), (1, -1)):
                origin = place(p, -b, -d)
                column(p, 4 + 4 * b + index, origin, tile).wait_recv()
                send(column(p, 6 + 4 * b + index, origin, place(p, 0, d)))

        def col_end(p):
            column_all(p, 6, SIDE).wait_recv()

        def multiply(f, start, wide, first, last):
            ks = pl.ds(start, wide)

            def step(i, _):
                part = pl.ds(pl.multiple_of(i * (units // 2), 16), units // 2)
                gram = lax.dot_general(rp[f][part, ks], cp[f][:, ks], (((1,), (1,)), ((), ())),
                                       preferred_element_type=jnp.float32)
                if start > 0:
                    gram = outs[f][part] + gram
                if start + wide == tokens:
                    gram = gram * (1.0 / tokens)
                outs[f][part] = gram
                return 0

            lax.fori_loop(first, last, step, 0)

        def each(act, pair, *more):
            for p in pairs[pair]:
                act(p, *more)

        lax.fori_loop(0, units // 128, make_hidden, 0)
        pl.semaphore_wait(barrier, len(peers))
        start_swap(0)
        build_perm()
        lax.fori_loop(0, units // 128, make_dgate, 0)
        end_swap(0)
        start_swap(1)
        for p in pairs[0]:
            pack(p)
            col_first(p)
        each(col_second, 0)
        each(col_near, 0)
        each(col_pass, 0, 0)
        end_swap(1)
        start_swap(2)
        for p in pairs[1]:
            pack(p)
            col_first(p)
        each(col_far, 0)
        each(col_second, 1)
        each(col_pass, 0, 1)
        each(col_near, 1)
        each(col_pass, 0, 3)
        each(col_pass, 0, 2)
        end_swap(2)
        row_out(0)
        for p in pairs[2]:
            pack(p)
            col_first(p)
        each(col_second, 2)
        each(col_pass, 1, 0)
        each(col_far, 1)
        each(pack, 3)
        each(col_near, 2)
        each(col_pass, 1, 1)
        row_pass(0)
        each(col_first, 3)
        each(col_pass, 1, 3)
        each(col_second, 3)
        each(col_pass, 1, 2)
        row_far(0)
        row_out(1)
        each(col_near, 3)
        row_end(0)
        each(col_pass, 2, 0)
        each(col_far, 2)
        each(col_end, 0)
        each(col_end, 1)
        multiply(0, 0, tokens, 0, 1)
        each(col_pass, 2, 1)
        row_pass(1)
        each(col_far, 3)
        each(col_pass, 2, 3)
        multiply(0, 0, tokens, 1, 2)
        each(col_pass, 2, 2)
        row_far(1)
        each(col_pass, 3, 0)
        each(col_pass, 3, 1)
        each(col_pass, 3, 3)
        row_end(1)
        each(col_pass, 3, 2)
        each(col_end, 2)
        multiply(1, 0, 2 * F1_WIDTHS[0], 0, 2)
        each(col_end, 3)
        for part in range(len(parts)):
            swap_all(part).wait_send()
        for f in range(2):
            row_sent(f)
        for p in range(len(pieces)):
            column_all(p, 0, 15).wait_send()

    vmem = pltpu.VMEM
    outputs = [
        vmem((units, columns), jnp.float32),
        vmem((units, columns), jnp.float32),
        vmem((units, tokens), jnp.bfloat16),
        vmem((columns, tokens), jnp.bfloat16),
    ]
    scratch = [vmem((capacity, units), jnp.bfloat16)] * 3 + [
        vmem((2, units, capacity), jnp.bfloat16),
        vmem((2, shards, group, capacity), jnp.bfloat16),
        vmem((len(slots), capacity, WIDE), jnp.bfloat16),
        vmem((units, tokens), jnp.bfloat16),
        vmem((columns, tokens), jnp.bfloat16),
        pltpu.SemaphoreType.DMA((3, units // 128)),
        pltpu.SemaphoreType.DMA((len(parts),)),
        pltpu.SemaphoreType.DMA((len(parts),)),
        pltpu.SemaphoreType.DMA((len(parts),)),
        pltpu.SemaphoreType.DMA((2,)),
        pltpu.SemaphoreType.DMA((2, 8)),
        pltpu.SemaphoreType.DMA((len(pieces),)),
        pltpu.SemaphoreType.DMA((len(pieces), 12)),
    ]
    return kernel, outputs, scratch


def make_finish(units, columns, tokens):
    last = 2 * sum(F1_WIDTHS[1:])

    def finish(act_in, grad_in, rp, cp, act_ref, grad_ref, total, act_s, grad_s):
        act_out = pltpu.make_async_copy(act_in, act_ref.at[:, 0, :], act_s)
        act_out.start()

        def half(i):
            return pl.ds(pl.multiple_of(i * (units // 2), 16), units // 2)

        def copy(i):
            return pltpu.make_async_copy(total.at[half(i)], grad_ref.at[half(i), 0, :], grad_s.at[i])

        def step(i, _):
            ks = pl.ds(tokens - last, last)
            gram = lax.dot_general(rp[half(i), ks], cp[:, ks], (((1,), (1,)), ((), ())),
                                   preferred_element_type=jnp.float32)
            total[half(i)] = (grad_in[half(i)] + gram) * (1.0 / tokens)
            copy(i).start()
            return 0

        lax.fori_loop(0, 2, step, 0)
        for i in range(2):
            copy(i).wait()
        act_out.wait()

    scratch = [
        pltpu.VMEM((units, columns), jnp.float32),
        pltpu.SemaphoreType.DMA,
        pltpu.SemaphoreType.DMA((2,)),
    ]
    return finish, scratch


def solution(mesh):
    shards, tiles = mesh.shape["dp"], mesh.shape["tile"]

    def on_device(gate_pre, up_pre, grad_hidden, doc_tokens, doc_shard):
        capacity, units = gate_pre.shape
        group = units // shards
        columns = tiles * group
        kernel, outputs, scratch = make_kernel(capacity, units, group, shards, tiles)
        smem, vmem = pl.BlockSpec(memory_space=pltpu.SMEM), pl.BlockSpec(memory_space=pltpu.VMEM)
        hbm = pl.BlockSpec(memory_space=pltpu.HBM)
        panels = pl.pallas_call(
            kernel,
            out_shape=outputs,
            in_specs=[smem, smem, hbm, hbm, hbm],
            out_specs=[vmem] * len(outputs),
            scratch_shapes=scratch,
            compiler_params=pltpu.CompilerParams(
                collective_id=0, has_side_effects=True, vmem_limit_bytes=30 << 20),
            name="gram_exchange",
        )(*(pltpu.with_memory_space_constraint(v, pltpu.HBM)
            for v in (doc_tokens, doc_shard, gate_pre, up_pre, grad_hidden)))
        finish, scratch = make_finish(units, columns, TOK_DEV * shards)
        anywhere = pl.BlockSpec(memory_space=pl.ANY)
        act, grad = pl.pallas_call(
            finish,
            out_shape=[jax.ShapeDtypeStruct((units, 1, columns), jnp.float32)] * 2,
            in_specs=[vmem] * len(outputs),
            out_specs=[anywhere] * 2,
            scratch_shapes=scratch,
            compiler_params=pltpu.CompilerParams(vmem_limit_bytes=16 << 20),
            name="gram_finish",
        )(*panels)
        return act, grad

    return jax.shard_map(
        on_device,
        mesh=mesh,
        in_specs=(P("dp", "tile"), P("dp", "tile"), P("dp", "tile"), P(), P()),
        out_specs=(P("tile", "dp", None), P("tile", "dp", None)),
        check_vma=False,
    )
```

```python
import jax
import jax.numpy as jnp
from jax import lax
from jax.experimental import pallas as pl
from jax.experimental.pallas import tpu as pltpu
from jax.sharding import PartitionSpec as P

MESH = pl.DeviceIdType.MESH
TOK_DEV = 256
DOCS_SHARD = 4
F1_WIDTHS = (512, 512)
WIDE = 256
SIDE = 4


def packing_blocks(shards, capacity, tokens):
    blocks = [[] for _ in range(tokens // WIDE)]
    for shard in range(shards):
        after = shards - shard
        first = max(DOCS_SHARD * shard, tokens - capacity * after)
        last = min(capacity * shard, tokens - DOCS_SHARD * after) + capacity
        for block in range(first // WIDE, -(-min(last, tokens) // WIDE)):
            blocks[block].append(shard)
    return blocks


def make_kernel(capacity, units, group, shards, tiles):
    tokens = TOK_DEV * shards
    blocks = packing_blocks(shards, capacity, tokens)
    slots = {}
    for n, members in enumerate(blocks):
        for shard in members:
            slots[n, shard] = len(slots)
    half = tokens // 2
    cut = group * 2 // 7
    parts = [(0, 0, cut), (0, cut, group - cut), (1, 0, group)]
    pieces = []
    for f, top, rows in parts[:2]:
        pieces += [(f, top, rows, 0, half), (f, top, rows, half, half)]
    start = 0
    for wide in F1_WIDTHS:
        pieces += [(1, 0, group, start, wide), (1, 0, group, start + wide, wide)]
        start += 2 * wide
    pairs = [(i, i + 1) for i in range(0, len(pieces), 2)]
    columns = tiles * group

    def kernel(tok_ref, own_ref, gate_hbm, up_hbm, down_hbm, act_ref, grad_ref, rp1, cp1,
               gate_ref, up_ref, down_ref, xt, rv, perm, rp0, cp0, load_s,
               swap_s, swap_r, local_s, row_s, row_r, col_s, col_r):
        outs, rp, cp = (act_ref, grad_ref), (rp0, rp1), (cp0, cp1)

        def send(copy):
            copy.start()

        def fetch(i, b):
            cols = pl.ds(pl.multiple_of(b * 128, 128), 128)
            source = (gate_hbm, up_hbm, down_hbm)[i]
            target = (gate_ref, up_ref, down_ref)[i]
            return pltpu.make_async_copy(source.at[:, cols], target.at[:, cols], load_s.at[i, b])

        def fetch_pair(b, _):
            fetch(0, b).start()
            fetch(1, b).start()
            return 0

        def fetch_down(b, _):
            fetch(2, b).start()
            return 0

        lax.fori_loop(0, units // 128, fetch_pair, 0)
        lax.fori_loop(0, units // 128, fetch_down, 0)

        dp, tile = lax.axis_index("dp"), lax.axis_index("tile")
        y, core = dp // 2, lax.rem(dp, 2)
        z, x = tile // SIDE, lax.rem(tile, SIDE)

        def plus(a, d):
            return lax.rem(a + d + SIDE, SIDE)

        def over_dp(offset):
            return lax.rem(dp + offset + shards, shards)

        def y_peer(d):
            return (plus(y, d) * 2 + core, tile)

        sibling = (y * 2 + 1 - core, tile)

        def plane(first_is_x, d1, d2):
            dx, dz = (d1, d2) if first_is_x else (d2, d1)
            return plus(z, dz) * SIDE + plus(x, dx)

        barrier = pltpu.get_barrier_semaphore()
        peers = [(over_dp(o), tile) for o in range(1, shards)]
        peers += [(dp, plane(True, d, 0)) for d in (1, 2, 3)] + [(dp, plane(True, 0, d)) for d in (1, 2, 3)]
        for peer in peers:
            pl.semaphore_signal(barrier, inc=1, device_id=peer, device_id_type=MESH)

        def count(i, loads):
            return tuple(v + jnp.where(own_ref[i] == j, tok_ref[i], 0) for j, v in enumerate(loads))

        loads = lax.fori_loop(0, shards * DOCS_SHARD, count, (jnp.int32(0),) * shards)
        own_load, offsets, total = jnp.int32(0), [], jnp.int32(0)
        for j in range(shards):
            own_load = own_load + jnp.where(dp == j, loads[j], 0)
            offsets.append(total)
            total = total + loads[j]

        live = lax.broadcasted_iota(jnp.int32, (capacity, 128), 0) < own_load

        def make_hidden(b, _):
            fetch(0, b).wait()
            fetch(1, b).wait()
            cols = pl.ds(pl.multiple_of(b * 128, 128), 128)
            g = gate_ref[:, cols].astype(jnp.float32)
            u = up_ref[:, cols].astype(jnp.float32)
            h = jnp.where(live, g * jax.nn.sigmoid(g) * u, 0.0)
            xt[0, cols, :] = h.T.astype(jnp.bfloat16)
            return 0

        def make_dgate(b, _):
            fetch(2, b).wait()
            cols = pl.ds(pl.multiple_of(b * 128, 128), 128)
            g = gate_ref[:, cols].astype(jnp.float32)
            u = up_ref[:, cols].astype(jnp.float32)
            d = down_ref[:, cols].astype(jnp.float32)
            s = jax.nn.sigmoid(g)
            h = jnp.where(live, d * u * s * (1.0 + g * (1.0 - s)), 0.0)
            xt[1, cols, :] = h.T.astype(jnp.bfloat16)
            return 0

        def at_group(index):
            return pl.ds(pl.multiple_of(index * group, 16), group)

        def rows_of(index, top, rows):
            return pl.ds(pl.multiple_of(index * group + top, 16), rows)

        def swap(part, o):
            f, top, rows = parts[part]
            return pltpu.make_async_remote_copy(
                src_ref=xt.at[f, rows_of(over_dp(o), top, rows)], dst_ref=rv.at[f, dp, pl.ds(top, rows)],
                send_sem=swap_s.at[part], recv_sem=swap_r.at[part],
                device_id=(over_dp(o), tile), device_id_type=MESH)

        def swap_all(part):
            f, top, rows = parts[part]
            both = rv.at[f, pl.ds(0, shards - 1), pl.ds(top, rows)]
            return pltpu.make_async_remote_copy(
                src_ref=both, dst_ref=both, send_sem=swap_s.at[part], recv_sem=swap_r.at[part],
                device_id=(over_dp(1), tile), device_id_type=MESH)

        def swap_own(part):
            f, top, rows = parts[part]
            return pltpu.make_async_copy(
                xt.at[f, rows_of(dp, top, rows)], rv.at[f, dp, pl.ds(top, rows)], local_s.at[part])

        def start_swap(part):
            for o in (3, 4, 5, 2, 6, 7, 1):
                swap(part, o).start()
            swap_own(part).start()

        def end_swap(part):
            swap_own(part).wait()
            swap_all(part).wait_recv()

        def build_perm():
            diff = (lax.broadcasted_iota(jnp.int32, (capacity, WIDE), 1)
                    - lax.broadcasted_iota(jnp.int32, (capacity, WIDE), 0))
            for (n, shard), slot in slots.items():
                hit = diff == offsets[shard] - n * WIDE
                perm[slot] = jnp.where(hit, 1.0, 0.0).astype(jnp.bfloat16)

        def pack(piece):
            f, top, rows, start, wide = pieces[piece]
            for n in range(start // WIDE, (start + wide) // WIDE):
                acc = None
                for shard in blocks[n]:
                    term = jnp.dot(rv[f, shard, top:top + rows], perm[slots[n, shard]],
                                   preferred_element_type=jnp.float32)
                    acc = term if acc is None else acc + term
                packed = acc.astype(jnp.bfloat16)
                cp[f][rows_of(tile, top, rows), n * WIDE:(n + 1) * WIDE] = packed
                rp[f][rows_of(dp, top, rows), n * WIDE:(n + 1) * WIDE] = packed

        def row(f, index, origin, peer):
            lanes = pl.ds((index - 2) * half, half) if index in (2, 3) else slice(None)
            part = rp[f].at[at_group(origin), lanes]
            return pltpu.make_async_remote_copy(
                src_ref=part, dst_ref=part, send_sem=row_s.at[f], recv_sem=row_r.at[f, index],
                device_id=peer, device_id_type=MESH)

        def same_core(d):
            return plus(y, d) * 2 + core

        def row_out(f):
            send(row(f, 0, dp, y_peer(1)))
            send(row(f, 1, dp, y_peer(-1)))
            send(row(f, 4, dp, sibling))

        def row_pass(f):
            for index, d in ((0, 1), (1, -1)):
                row(f, index, same_core(-d), sibling).wait_recv()
                send(row(f, 2 + index, same_core(-d), y_peer(d)))
                send(row(f, 5 + index, same_core(-d), sibling))

        def row_far(f):
            for index in (2, 3):
                row(f, index, same_core(2), sibling).wait_recv()
            send(row(f, 7, same_core(2), sibling))

        def row_sent(f):
            whole = rp[f].at[pl.ds(0, 7 * group)]
            pltpu.make_async_remote_copy(
                src_ref=whole, dst_ref=whole, send_sem=row_s.at[f], recv_sem=row_r.at[f, 0],
                device_id=sibling, device_id_type=MESH).wait_send()

        def row_end(f):
            for index, d in ((4, 0), (5, -1), (6, 1), (7, 2)):
                row(f, index, plus(y, d) * 2 + 1 - core, sibling).wait_recv()

        def arrival(index):
            kind, b = index % 4, index // 4
            if kind < 2:
                return 2 * b + kind
            return 10 if b == 0 else 11

        def column(piece, index, origin, peer):
            f, top, rows, start, wide = pieces[piece]
            kind = index % 4
            if kind >= 2:
                wide = wide // 2
                start += (kind - 2) * wide
            part = cp[f].at[rows_of(origin, top, rows), pl.ds(start, wide)]
            return pltpu.make_async_remote_copy(
                src_ref=part, dst_ref=part, send_sem=col_s.at[piece], recv_sem=col_r.at[piece, arrival(index)],
                device_id=(dp, peer), device_id_type=MESH)

        def column_all(piece, index, count):
            f, top, rows, start, wide = pieces[piece]
            part = cp[f].at[pl.ds(0, count * rows), pl.ds(start, wide)]
            return pltpu.make_async_remote_copy(
                src_ref=part, dst_ref=part, send_sem=col_s.at[piece], recv_sem=col_r.at[piece, arrival(index)],
                device_id=(dp, tile), device_id_type=MESH)

        def place(piece, d1, d2):
            return plane(piece % 2 == 0, d1, d2)

        def col_first(p):
            for index, d in ((0, 1), (1, -1)):
                send(column(p, index, tile, place(p, d, 0)))

        def col_second(p):
            for index, d in ((4, 1), (5, -1)):
                send(column(p, index, tile, place(p, 0, d)))

        def col_out(pair):
            each(col_first, pair)
            each(col_second, pair)

        def col_near(p):
            for index, d in ((0, 1), (1, -1)):
                origin = place(p, -d, 0)
                column(p, index, origin, tile).wait_recv()
                send(column(p, 2 + index, origin, place(p, d, 0)))
            for b, d in ((1, 1), (3, -1)):
                origin = place(p, -d, 0)
                send(column(p, 4 + 4 * b, origin, place(p, 0, 1)))
                send(column(p, 5 + 4 * b, origin, place(p, 0, -1)))

        def col_far(p):
            origin = place(p, 2, 0)
            column_all(p, 2, 1).wait_recv()
            send(column(p, 12, origin, place(p, 0, 1)))
            send(column(p, 13, origin, place(p, 0, -1)))

        def col_pass(p, b):
            for index, d in ((0, 1), (1, -1)):
                origin = place(p, -b, -d)
                column(p, 4 + 4 * b + index, origin, tile).wait_recv()
                send(column(p, 6 + 4 * b + index, origin, place(p, 0, d)))

        def col_end(p):
            column_all(p, 6, SIDE).wait_recv()

        def multiply(f, start, wide, first, last):
            ks = pl.ds(start, wide)

            def step(i, _):
                part = pl.ds(pl.multiple_of(i * (units // 2), 16), units // 2)
                gram = lax.dot_general(rp[f][part, ks], cp[f][:, ks], (((1,), (1,)), ((), ())),
                                       preferred_element_type=jnp.float32)
                if start > 0:
                    gram = outs[f][part] + gram
                if start + wide == tokens:
                    gram = gram * (1.0 / tokens)
                outs[f][part] = gram
                return 0

            lax.fori_loop(first, last, step, 0)

        def each(act, pair, *more):
            for p in pairs[pair]:
                act(p, *more)

        lax.fori_loop(0, units // 128, make_hidden, 0)
        pl.semaphore_wait(barrier, len(peers))
        start_swap(0)
        build_perm()
        lax.fori_loop(0, units // 128, make_dgate, 0)
        end_swap(0)
        start_swap(1)
        for p in pairs[0]:
            pack(p)
            col_first(p)
        each(col_second, 0)
        each(col_near, 0)
        each(col_pass, 0, 0)
        end_swap(1)
        start_swap(2)
        for p in pairs[1]:
            pack(p)
            col_first(p)
        each(col_far, 0)
        each(col_second, 1)
        each(col_pass, 0, 1)
        each(col_near, 1)
        each(col_pass, 0, 3)
        each(col_pass, 0, 2)
        end_swap(2)
        row_out(0)
        for p in pairs[2]:
            pack(p)
            col_first(p)
        each(col_second, 2)
        each(col_pass, 1, 0)
        each(col_far, 1)
        each(pack, 3)
        each(col_near, 2)
        each(col_pass, 1, 1)
        row_pass(0)
        each(col_first, 3)
        each(col_pass, 1, 3)
        each(col_second, 3)
        each(col_pass, 1, 2)
        row_far(0)
        row_out(1)
        each(col_near, 3)
        row_end(0)
        each(col_pass, 2, 0)
        each(col_far, 2)
        each(col_end, 0)
        each(col_end, 1)
        multiply(0, 0, tokens, 0, 1)
        each(col_pass, 2, 1)
        row_pass(1)
        each(col_far, 3)
        each(col_pass, 2, 3)
        multiply(0, 0, tokens, 1, 2)
        each(col_pass, 2, 2)
        row_far(1)
        each(col_pass, 3, 0)
        each(col_pass, 3, 1)
        each(col_pass, 3, 3)
        row_end(1)
        each(col_pass, 3, 2)
        each(col_end, 2)
        multiply(1, 0, 2 * F1_WIDTHS[0], 0, 2)
        each(col_end, 3)
        for part in range(len(parts)):
            swap_all(part).wait_send()
        for f in range(2):
            row_sent(f)
        for p in range(len(pieces)):
            column_all(p, 0, 15).wait_send()

    vmem = pltpu.VMEM
    outputs = [
        vmem((units, columns), jnp.float32),
        vmem((units, columns), jnp.float32),
        vmem((units, tokens), jnp.bfloat16),
        vmem((columns, tokens), jnp.bfloat16),
    ]
    scratch = [vmem((capacity, units), jnp.bfloat16)] * 3 + [
        vmem((2, units, capacity), jnp.bfloat16),
        vmem((2, shards, group, capacity), jnp.bfloat16),
        vmem((len(slots), capacity, WIDE), jnp.bfloat16),
        vmem((units, tokens), jnp.bfloat16),
        vmem((columns, tokens), jnp.bfloat16),
        pltpu.SemaphoreType.DMA((3, units // 128)),
        pltpu.SemaphoreType.DMA((len(parts),)),
        pltpu.SemaphoreType.DMA((len(parts),)),
        pltpu.SemaphoreType.DMA((len(parts),)),
        pltpu.SemaphoreType.DMA((2,)),
        pltpu.SemaphoreType.DMA((2, 8)),
        pltpu.SemaphoreType.DMA((len(pieces),)),
        pltpu.SemaphoreType.DMA((len(pieces), 12)),
    ]
    return kernel, outputs, scratch


def make_finish(units, columns, tokens):
    last = 2 * sum(F1_WIDTHS[1:])

    def finish(act_in, grad_in, rp, cp, act_ref, grad_ref, total, act_s, grad_s):
        act_out = pltpu.make_async_copy(act_in, act_ref.at[:, 0, :], act_s)
        act_out.start()

        ks = pl.ds(tokens - last, last)
        copies = []
        for first, wide in ((0, 3 * WIDE), (3 * WIDE, 2 * WIDE), (5 * WIDE, 2 * WIDE)):
            cols = pl.ds(first, wide)
            gram = lax.dot_general(rp[:, ks], cp[cols, ks], (((1,), (1,)), ((), ())),
                                   preferred_element_type=jnp.float32)
            total[:, cols] = (grad_in[:, cols] + gram) * (1.0 / tokens)
            copies.append(pltpu.make_async_copy(
                total.at[:, cols], grad_ref.at[:, 0, cols], grad_s.at[len(copies)]))
            copies[-1].start()
        for copy in copies:
            copy.wait()
        act_out.wait()

    scratch = [
        pltpu.VMEM((units, columns), jnp.float32),
        pltpu.SemaphoreType.DMA,
        pltpu.SemaphoreType.DMA((3,)),
    ]
    return finish, scratch


def solution(mesh):
    shards, tiles = mesh.shape["dp"], mesh.shape["tile"]

    def on_device(gate_pre, up_pre, grad_hidden, doc_tokens, doc_shard):
        capacity, units = gate_pre.shape
        group = units // shards
        columns = tiles * group
        kernel, outputs, scratch = make_kernel(capacity, units, group, shards, tiles)
        smem, vmem = pl.BlockSpec(memory_space=pltpu.SMEM), pl.BlockSpec(memory_space=pltpu.VMEM)
        hbm = pl.BlockSpec(memory_space=pltpu.HBM)
        panels = pl.pallas_call(
            kernel,
            out_shape=outputs,
            in_specs=[smem, smem, hbm, hbm, hbm],
            out_specs=[vmem] * len(outputs),
            scratch_shapes=scratch,
            compiler_params=pltpu.CompilerParams(
                collective_id=0, has_side_effects=True, vmem_limit_bytes=30 << 20),
            name="gram_exchange",
        )(*(pltpu.with_memory_space_constraint(v, pltpu.HBM)
            for v in (doc_tokens, doc_shard, gate_pre, up_pre, grad_hidden)))
        finish, scratch = make_finish(units, columns, TOK_DEV * shards)
        anywhere = pl.BlockSpec(memory_space=pl.ANY)
        act, grad = pl.pallas_call(
            finish,
            out_shape=[jax.ShapeDtypeStruct((units, 1, columns), jnp.float32)] * 2,
            in_specs=[vmem] * len(outputs),
            out_specs=[anywhere] * 2,
            scratch_shapes=scratch,
            compiler_params=pltpu.CompilerParams(vmem_limit_bytes=16 << 20),
            name="gram_finish",
        )(*panels)
        return act, grad

    return jax.shard_map(
        on_device,
        mesh=mesh,
        in_specs=(P("dp", "tile"), P("dp", "tile"), P("dp", "tile"), P(), P()),
        out_specs=(P("tile", "dp", None), P("tile", "dp", None)),
        check_vma=False,
    )
```
